32 devices in a mesh: dp: 4 (over y, x), seq: 8 (over z, core).
Axes of the slice: x: 2, y: 2, z: 4, core: 2. Of those that a mesh axis runs over, the one named last changes fastest.
Arguments:
- queries: bfloat16 [4, 2048, 1024], P('dp', 'seq'), may hold values from -7.5 to 7.5
- keys: bfloat16 [4, 2048, 1024], P('dp', 'seq'), may hold values from -7.5 to 7.5
- values: bfloat16 [4, 2048, 1024], P('dp', 'seq'), may hold values from -7.5 to 7.5
- grad_out: bfloat16 [4, 2048, 1024], P('dp', 'seq'), may hold values from -3 to 3
- w_out: bfloat16 [1024, 1024], replicated, may hold values from -0.1875 to 0.1875
Outputs:
- mixed: bfloat16 [4, 2048, 1024], P('dp', 'seq')
- grad_queries: bfloat16 [4, 2048, 1024], P('dp', 'seq')
- grad_keys: bfloat16 [4, 2048, 1024], P('dp', 'seq')
- grad_values: bfloat16 [4, 2048, 1024], P('dp', 'seq')
- grad_w_out: float32 [1024, 1024], P(('dp', 'seq'))
The draws below stay inside these ranges and needn't reach their ends.
All inputs are finite; a program needn't handle non-finite values.
Results may differ from the reference program's by a relative error of at most 0.03.
Values may be sent and summed in bfloat16 or wider, within the bound.
No kernel may reach another device: no remote copies, remote signals or barrier semaphores. Data moves between devices by JAX's collectives and lax.ppermute only.
A program may use at most 128 MiB of HBM per device.

```python
import math
import jax
import jax.numpy as jnp
from jax import lax

HEADS = 8
HEAD_DIM = 128
D = 1024
BLOCK = 128
TOK_DEV = 256
LEVELS = 4
SEQ_LEN = 2048
SEQS = 4


def segment_field(key, gain, region_gain):
    segment = BLOCK // 2
    means = jax.random.normal(jax.random.fold_in(key, 1), (SEQS, SEQ_LEN // segment, D), jnp.float32)
    regions = jax.random.normal(jax.random.fold_in(key, 3), (SEQS, SEQ_LEN // TOK_DEV, D), jnp.float32)
    noise = jax.random.normal(jax.random.fold_in(key, 2), (SEQS, SEQ_LEN, D), jnp.float32)
    field = gain * (jnp.repeat(means, segment, axis=1) + noise) + region_gain * jnp.repeat(regions, TOK_DEV, axis=1)
    return jnp.clip(field, -7.5, 7.5)


def drawn_pair(key):
    query_field = segment_field(jax.random.fold_in(key, 101), 0.6, 0.0)
    key_field = segment_field(jax.random.fold_in(key, 202), 0.6, 0.0)
    return (query_field, key_field)


def draw_queries(key, part):
    return drawn_pair(key)[0].astype(jnp.bfloat16)


def draw_keys(key, part):
    return drawn_pair(key)[1].astype(jnp.bfloat16)


def draw_values(key, part):
    return segment_field(jax.random.fold_in(key, 404), 1.0, 1.5).astype(jnp.bfloat16)


def block_levels(key, extent, split, low, largest):
    level = 1.0
    for axis_at, shards_of in split:
        heights = jax.random.uniform(jax.random.fold_in(jax.random.fold_in(key, 6), axis_at), (shards_of,), jnp.float32, low / len(split), largest / len(split))
        level = level * jnp.repeat(jnp.exp(heights), extent[axis_at] // shards_of).reshape((-1,) + (1,) * (len(extent) - 1 - axis_at))
    return level


def normal_values(own_key, extent, scale, reach, shards=(), held_as=jnp.bfloat16):
    drawn = jax.random.normal(own_key, extent, jnp.float32) * scale
    if len(shards) > 0:
        drawn = block_levels(own_key, extent, shards, -0.22, 0.18) * drawn
    return jnp.clip(drawn, min=-reach, max=reach).astype(held_as)


def setup_inputs(seed: int = 0) -> dict:
    splits = jax.random.split(jax.random.key(seed), 6)
    queries = draw_queries(jax.random.fold_in(splits[5], 71), 0)
    keys = draw_keys(jax.random.fold_in(splits[5], 71), 0)
    values = draw_values(jax.random.fold_in(splits[5], 71), 0)
    grad_out = normal_values(splits[3], (SEQS, SEQ_LEN, D), 0.5, 3.0, ((0, 4), (1, 8)))
    w_out = normal_values(splits[4], (D, D), D ** -0.5, 0.1875)
    return {"queries": queries, "keys": keys, "values": values, "grad_out": grad_out, "w_out": w_out}


LOG_TWO = math.log(2.0)

def pooled(rows):
    shape = rows.shape
    pairs = rows.astype(jnp.float32).reshape(shape[:-2] + (shape[-2] // 2, 2, shape[-1]))
    return ((pairs[..., 0, :] + pairs[..., 1, :]) * 0.5).astype(jnp.bfloat16)

def sibling(blocks):
    count = blocks.shape[0]
    return jnp.flip(blocks.reshape((count // 2, 2) + blocks.shape[1:]), axis=1).reshape(blocks.shape)

def grouped(per_token, groups):
    return jnp.transpose(per_token.reshape(groups, -1, per_token.shape[-1]), (0, 2, 1))

def ungrouped(blocks):
    return jnp.transpose(blocks, (0, 2, 1)).reshape(-1, blocks.shape[1])

def widened(narrow):
    return lax.optimization_barrier(narrow).astype(jnp.float32)

def level_blocks(level, query_rows, key_rows, value_rows):
    if level == 0:
        shape = (query_rows.shape[0] // (2 * BLOCK), 2 * BLOCK, HEADS, HEAD_DIM)
        return (query_rows.reshape(shape), key_rows.reshape(shape), value_rows.reshape(shape))
    shape = (query_rows.shape[0] // BLOCK, BLOCK, HEADS, HEAD_DIM)
    return (query_rows.reshape(shape), sibling(key_rows.reshape(shape)), sibling(value_rows.reshape(shape)))

def level_scores(level, query_blocks, key_blocks):
    scale = 1.0 / math.sqrt(HEAD_DIM)
    scores = jnp.einsum('gqhd,gkhd->ghqk', query_blocks.astype(jnp.float32), key_blocks.astype(jnp.float32))
    return jnp.repeat(scores * scale + level * LOG_TWO, 2 ** level, axis=2)

def one_sequence(query_tok, key_tok, value_tok, grad_tok, w_out):
    scale = 1.0 / math.sqrt(HEAD_DIM)
    pyramid = [(query_tok, key_tok, value_tok)]
    for level in range(1, LEVELS):
        previous = pyramid[-1]
        pyramid.append((pooled(previous[0]), pooled(previous[1]), pooled(previous[2])))
    top = None
    for level in range(LEVELS):
        query_blocks, key_blocks, value_blocks = level_blocks(level, *pyramid[level])
        row_top = ungrouped(lax.optimization_barrier(jnp.max(level_scores(level, query_blocks, key_blocks), axis=3)))
        top = row_top if top is None else jnp.maximum(top, row_top)
    numer = jnp.zeros((SEQ_LEN, HEADS, HEAD_DIM), jnp.float32)
    denom = jnp.zeros((SEQ_LEN, HEADS), jnp.float32)
    for level in range(LEVELS):
        query_blocks, key_blocks, value_blocks = level_blocks(level, *pyramid[level])
        scores = level_scores(level, query_blocks, key_blocks)
        groups = scores.shape[0]
        expo = jnp.exp(scores - grouped(top, groups)[..., None])
        term = jnp.einsum('ghrk,gkhd->grhd', widened(expo.astype(jnp.bfloat16)), value_blocks.astype(jnp.float32))
        numer = numer + term.reshape(SEQ_LEN, HEADS, HEAD_DIM)
        denom = denom + ungrouped(lax.optimization_barrier(jnp.sum(expo, axis=3)))
    attended = (numer / denom[:, :, None]).reshape(SEQ_LEN, D).astype(jnp.bfloat16)
    mixed = jnp.dot(attended, w_out, preferred_element_type=jnp.float32).astype(jnp.bfloat16)
    grad_att = jnp.dot(grad_tok, w_out.T, preferred_element_type=jnp.float32).astype(jnp.bfloat16)
    weight_term = jnp.dot(attended.T, grad_tok, preferred_element_type=jnp.float32)
    delta = lax.optimization_barrier(jnp.sum(grad_att.astype(jnp.float32).reshape(SEQ_LEN, HEADS, HEAD_DIM) * attended.astype(jnp.float32).reshape(SEQ_LEN, HEADS, HEAD_DIM), axis=2))
    query_grads = [jnp.zeros((SEQ_LEN // 2 ** level, D), jnp.float32) for level in range(LEVELS)]
    key_grads = [jnp.zeros((SEQ_LEN // 2 ** level, D), jnp.float32) for level in range(LEVELS)]
    value_grads = [jnp.zeros((SEQ_LEN // 2 ** level, D), jnp.float32) for level in range(LEVELS)]
    for level in range(LEVELS):
        query_blocks, key_blocks, value_blocks = level_blocks(level, *pyramid[level])
        scores = level_scores(level, query_blocks, key_blocks)
        groups = scores.shape[0]
        prob = jnp.exp(scores - grouped(top, groups)[..., None]) / grouped(denom, groups)[..., None]
        grad_rows = grad_att.reshape(groups, -1, HEADS, HEAD_DIM).astype(jnp.float32)
        value_grad = jnp.einsum('ghrk,grhd->gkhd', widened(prob.astype(jnp.bfloat16)), grad_rows)
        prob_grad = jnp.einsum('grhd,gkhd->ghrk', grad_rows, value_blocks.astype(jnp.float32))
        score_grad = prob * (prob_grad - grouped(delta, groups)[..., None])
        summed = score_grad.reshape(groups, HEADS, -1, 2 ** level, score_grad.shape[3]).sum(axis=3)
        summed = widened(summed.astype(jnp.bfloat16))
        query_grad = jnp.einsum('ghqk,gkhd->gqhd', summed, key_blocks.astype(jnp.float32)) * scale
        key_grad = jnp.einsum('ghqk,gqhd->gkhd', summed, query_blocks.astype(jnp.float32)) * scale
        if level > 0:
            key_grad = sibling(key_grad)
            value_grad = sibling(value_grad)
        query_grads[level] = query_grads[level] + query_grad.reshape(-1, D)
        key_grads[level] = key_grads[level] + key_grad.reshape(-1, D)
        value_grads[level] = value_grads[level] + value_grad.reshape(-1, D)
    for level in range(LEVELS - 1, 0, -1):
        query_grads[level - 1] = query_grads[level - 1] + 0.5 * jnp.repeat(query_grads[level], 2, axis=0)
        key_grads[level - 1] = key_grads[level - 1] + 0.5 * jnp.repeat(key_grads[level], 2, axis=0)
        value_grads[level - 1] = value_grads[level - 1] + 0.5 * jnp.repeat(value_grads[level], 2, axis=0)
    return (mixed, query_grads[0].astype(jnp.bfloat16), key_grads[0].astype(jnp.bfloat16), value_grads[0].astype(jnp.bfloat16), weight_term)

def reference(queries, keys, values, grad_out, w_out):
    results = []
    for sequence in range(SEQS):
        results.append(one_sequence(queries[sequence], keys[sequence], values[sequence], grad_out[sequence], w_out))
    mixed = jnp.stack([item[0] for item in results])
    grad_queries = jnp.stack([item[1] for item in results])
    grad_keys = jnp.stack([item[2] for item in results])
    grad_values = jnp.stack([item[3] for item in results])
    weight_total = results[0][4]
    for item in results[1:]:
        weight_total = weight_total + item[4]
    grad_w_out = weight_total * (1.0 / math.sqrt(SEQS * SEQ_LEN))
    return (mixed, grad_queries, grad_keys, grad_values, grad_w_out)
```

```python
import functools
import math

import jax
import jax.numpy as jnp
from jax import lax
from jax.experimental import pallas as pl
from jax.experimental.pallas import tpu as pltpu
from jax.sharding import PartitionSpec as P

HEADS = 8
HEAD_DIM = 128
BLOCK = 128
LANES = 128
SCALE = 1.0 / math.sqrt(HEAD_DIM)
SCALE2 = SCALE / math.log(2.0)
F32 = jnp.float32
BF16 = jnp.bfloat16
VMEM_LIMIT = 48 * 1024 * 1024


def dot(a, b, dims):
    return lax.dot_general(a, b, (dims, ((), ())), preferred_element_type=F32)


def nn(a, b):
    return dot(a, b, ((1,), (0,)))


def nt(a, b):
    return dot(a, b, ((1,), (1,)))


def tn(a, b):
    return dot(a, b, ((0,), (0,)))


def member(rows, cols, row_shift, col_shift, value):
    r = lax.broadcasted_iota(jnp.int32, (rows, cols), 0) >> row_shift
    c = lax.broadcasted_iota(jnp.int32, (rows, cols), 1) >> col_shift
    return jnp.where(r == c, value, 0.0).astype(BF16)


def call(kernel, outs, name, flops, *operands):
    moved = sum(x.size * x.dtype.itemsize for x in operands)
    moved += sum(math.prod(s) * jnp.dtype(t).itemsize for s, t in outs)
    return pl.pallas_call(
        kernel,
        name=name,
        out_shape=[jax.ShapeDtypeStruct(s, t) for s, t in outs],
        in_specs=[pl.BlockSpec(memory_space=pltpu.VMEM)] * len(operands),
        out_specs=[pl.BlockSpec(memory_space=pltpu.VMEM)] * len(outs),
        compiler_params=pltpu.CompilerParams(vmem_limit_bytes=VMEM_LIMIT),
        cost_estimate=pl.CostEstimate(flops=flops, bytes_accessed=moved, transcendentals=0),
    )(*operands)


def pool_kernel(levels, k_ref, v_ref, *outs):
    tokens, width = k_ref.shape
    pools = [member(tokens >> l, tokens, 0, l, 0.5**l) for l in range(1, levels)]
    for which, src in enumerate((k_ref, v_ref)):
        x = src[...]
        for pool, out in zip(pools, outs):
            out[which] = nn(pool, x).astype(BF16)


def early_kernel(levels, q_ref, g_ref, w_ref, qhat_ref, ga_ref, *qls):
    tokens, width = q_ref.shape
    q = q_ref[...]
    for l in range(1, levels):
        qhat_ref[l - 1] = nn(member(tokens, tokens, l, l, 0.5**l), q).astype(BF16)
        qls[l - 1][...] = nn(member(tokens >> l, tokens, 0, l, 0.5**l), q).astype(BF16)
    g = g_ref[...]
    for c in range(0, width, 256):
        ga_ref[:, c : c + 256] = nt(g, w_ref[c : c + 256, :]).astype(BF16)


def forward_kernel(levels, pieces, dp, q_ref, k_ref, v_ref, qhat_ref, ga_ref, *refs):
    tokens, width = q_ref.shape
    upper = levels - 1
    count = sum(pieces)
    qls, refs = refs[:upper], refs[upper:]
    kvs, refs = refs[:count], refs[count:]
    e_ref, gr_ref, dd_ref, att_ref = refs[:4]
    blocks, msgs = refs[4 : 4 + dp], refs[4 + dp :]
    lane = lax.broadcasted_iota(jnp.int32, (tokens, LANES), 1)
    ones = jnp.ones((tokens + upper * BLOCK, LANES), BF16)
    sums = [member(tokens >> l, tokens, 0, l, 1.0) for l in range(1, levels)]
    aux = [jnp.zeros((tokens, LANES), F32) for _ in range(upper)]
    dd = jnp.zeros((tokens, LANES), F32)
    for h in range(HEADS):
        hs = slice(h * HEAD_DIM, (h + 1) * HEAD_DIM)
        keys, vals, at = [], [v_ref[:, hs]], 0
        for l in range(1, levels):
            part = kvs[at : at + pieces[l - 1]]
            at += pieces[l - 1]
            keys.append(jnp.concatenate([p[0, :, hs] for p in part], axis=0))
            vals.extend(p[1, :, hs] for p in part)
        raw0 = nt(q_ref[:, hs], k_ref[:, hs])
        raws = [nt(qhat_ref[l - 1, :, hs], keys[l - 1]) for l in range(1, levels)]
        top = jnp.max(raw0, axis=1, keepdims=True) * SCALE2
        mus = []
        for l in range(1, levels):
            big = jnp.max(raws[l - 1], axis=1, keepdims=True)
            top = jnp.maximum(top, big * SCALE2 + float(l))
            mus.append(big.astype(BF16).astype(F32))
        es = [jnp.exp2(raw0 * SCALE2 - top).astype(BF16)]
        for l in range(1, levels):
            es.append(jnp.exp2(raws[l - 1] * SCALE2 + (float(l) - top)).astype(BF16))
        e = jnp.concatenate(es, axis=1)
        e_ref[h] = e
        v_all = jnp.concatenate([jnp.concatenate(vals, axis=0), ones], axis=1)
        both = nn(e, v_all)
        rden = 1.0 / both[:, HEAD_DIM:]
        att = (both[:, :HEAD_DIM] * rden).astype(BF16)
        att_ref[:, hs] = att
        ga = ga_ref[:, hs].astype(F32)
        gr = ga * rden
        gr_ref[:, hs] = gr.astype(BF16)
        delta = jnp.sum(gr * att.astype(F32), axis=1, keepdims=True)
        dd = jnp.where(lane == h, delta, dd)
        for l in range(1, levels):
            a = jnp.exp2(mus[l - 1] * SCALE2 + (float(l) - top))
            n = tokens >> l
            msgs[l - 1][:, hs] = nn(sums[l - 1], (gr * a).astype(BF16)).astype(BF16)
            mixed = jnp.where(lane == h, mus[l - 1] * 0.5**l, aux[l - 1])
            aux[l - 1] = jnp.where(lane == HEADS + h, delta * a, mixed)
    dd_ref[...] = dd
    for l in range(1, levels):
        msgs[l - 1][:, width : 2 * width] = qls[l - 1][...]
        msgs[l - 1][:, 2 * width :] = nn(sums[l - 1], aux[l - 1].astype(BF16)).astype(BF16)
    me = lax.axis_index("dp")
    span = width // dp
    for m in range(dp):
        at = pl.multiple_of((me ^ m) * span, span)
        blocks[m][...] = att_ref[:, pl.ds(at, span)]


def backward_kernel(levels, pieces, e_ref, gr_ref, dd_ref, ga_ref, q_ref, k_ref, v_ref, *refs):
    tokens, width = q_ref.shape
    count = sum(pieces)
    kvs = refs[:count]
    att_ref, w_ref, gq_ref, dk_ref, dv_ref, mixed_ref, y_ref = refs[count:]
    upper = levels - 1
    for h in range(HEADS):
        hs = slice(h * HEAD_DIM, (h + 1) * HEAD_DIM)
        keys, vals, at = [], [v_ref[:, hs]], 0
        for l in range(1, levels):
            part = kvs[at : at + pieces[l - 1]]
            at += pieces[l - 1]
            keys.append(jnp.concatenate([p[0, :, hs] for p in part], axis=0))
            vals.extend(p[1, :, hs] for p in part)
        e = e_ref[h]
        gr = gr_ref[:, hs]
        dp_all = nt(gr, jnp.concatenate(vals, axis=0))
        ds = (e.astype(F32) * (dp_all - dd_ref[:, h : h + 1])).astype(BF16)
        dv_ref[:, hs] = tn(e[:, :tokens], gr).astype(BF16)
        dk_ref[:, hs] = (tn(ds[:, :tokens], q_ref[:, hs]) * SCALE).astype(BF16)
        gq_ref[:, hs] = nn(ds[:, :tokens], k_ref[:, hs])
        for l in range(1, levels):
            at = tokens + (l - 1) * BLOCK
            y_ref[(l - 1) * tokens : l * tokens, hs] = nn(
                ds[:, at : at + BLOCK], keys[l - 1]
            ).astype(BF16)
    spread = jnp.concatenate(
        [member(tokens, tokens, l, l, 0.5**l) for l in range(1, levels)], axis=1
    )
    for c in range(0, width, 256):
        cs = slice(c, c + 256)
        gq_ref[:, cs] = (gq_ref[:, cs] + nn(spread, y_ref[:, cs])) * SCALE
        mixed_ref[:, cs] = nn(att_ref[...], w_ref[:, cs]).astype(BF16)


def weight_kernel(dp, nz, *refs):
    atts, refs = refs[:dp], refs[dp:]
    grads, refs = refs[: dp], refs[dp:]
    keep_ref, send_ref, total_ref = refs
    a = jnp.concatenate([x[...] for x in atts], axis=0)
    width = grads[0].shape[1]
    for c in range(0, width, 256):
        cs = slice(c, c + 256)
        g = jnp.concatenate([x[:, cs] for x in grads], axis=0)
        total_ref[:, cs] = tn(a, g)
    rows = total_ref.shape[0] // (2 * nz)
    seq = lax.axis_index("seq")
    core, z = seq & 1, seq >> 1
    for m in range(nz):
        base = (z ^ m) * 2 * rows
        mine = pl.multiple_of(base + core * rows, rows)
        other = pl.multiple_of(base + (1 - core) * rows, rows)
        keep_ref[m * rows : (m + 1) * rows, :] = total_ref[pl.ds(mine, rows), :]
        send_ref[m * rows : (m + 1) * rows, :] = total_ref[pl.ds(other, rows), :].astype(BF16)


def halves_kernel(keep_ref, got_ref, *outs):
    rows = outs[0].shape[0]
    total = keep_ref[...] + got_ref[...].astype(F32)
    for m, out in enumerate(outs):
        out[...] = total[m * rows : (m + 1) * rows].astype(out.dtype)


def final_kernel(factor, *refs):
    out = refs[-1]
    total = refs[0][...]
    for x in refs[1:-1]:
        total = total + x[...].astype(F32)
    out[...] = total * factor


def owner_kernel(levels, pieces, tokens, *refs):
    upper = levels - 1
    count = sum(pieces)
    kvs, refs = refs[:upper], refs[upper:]
    msgs, refs = refs[:count], refs[count:]
    dk0_ref, dv0_ref, gk_ref, gv_ref, dks_ref, dvs_ref = refs
    width = dk0_ref.shape[1]
    auxes, at = [], 0
    groups = []
    for l in range(1, levels):
        part = msgs[at : at + pieces[l - 1]]
        at += pieces[l - 1]
        groups.append(part)
        auxes.append(jnp.concatenate([p[:, 2 * width :] for p in part], axis=0))
    for h in range(HEADS):
        hs = slice(h * HEAD_DIM, (h + 1) * HEAD_DIM)
        qs = slice(width + h * HEAD_DIM, width + (h + 1) * HEAD_DIM)
        at = 0
        for l in range(1, levels):
            n = tokens >> l
            lane = lax.broadcasted_iota(jnp.int32, (n, LANES), 1)
            minus_mu = jnp.where(lane == h, -1.0, 0.0).astype(BF16)
            minus_d = jnp.where(lane == HEADS + h, -1.0, 0.0).astype(BF16)
            ga = jnp.concatenate([p[:, hs] for p in groups[l - 1]], axis=0)
            q = jnp.concatenate([p[:, qs] for p in groups[l - 1]], axis=0)
            aux = auxes[l - 1]
            k = jnp.concatenate([kvs[l - 1][0, :, hs], minus_mu], axis=1)
            v = jnp.concatenate([kvs[l - 1][1, :, hs], minus_d], axis=1)
            e = jnp.exp2(nt(k, jnp.concatenate([q, aux], axis=1)) * SCALE2)
            ds = e * nt(v, jnp.concatenate([ga, aux], axis=1))
            dvs_ref[at : at + n, hs] = nn(e.astype(BF16), ga).astype(BF16)
            dks_ref[at : at + n, hs] = (nn(ds.astype(BF16), q) * SCALE).astype(BF16)
            at += n
    total = dks_ref.shape[0]
    spread = jnp.concatenate(
        [member(tokens, tokens >> l, l, 0, 0.5**l) for l in range(1, levels)], axis=1
    )
    for c in range(0, width, 256):
        cs = slice(c, c + 256)
        gk_ref[:, cs] = (dk0_ref[:, cs].astype(F32) + nn(spread, dks_ref[:, cs])).astype(BF16)
        gv_ref[:, cs] = (dv0_ref[:, cs].astype(F32) + nn(spread, dvs_ref[:, cs])).astype(BF16)


def swap(x, axis, mask):
    count = lax.axis_size(axis)
    return lax.ppermute(x, axis, [(i, i ^ mask) for i in range(count)])


def body(queries, keys, values, grad_out, w_out):
    seq = lax.axis_size("seq")
    dp = lax.axis_size("dp")
    nz = seq // 2
    levels = seq.bit_length()
    upper = levels - 1
    q, k, v, g = queries[0], keys[0], values[0], grad_out[0]
    tokens, width = q.shape
    factor = 1.0 / math.sqrt(dp * seq * tokens)

    own = call(
        functools.partial(pool_kernel, levels),
        [((2, tokens >> l, width), BF16) for l in range(1, levels)],
        "pool",
        2 * 2 * tokens * tokens * width,
        k,
        v,
    )

    def exchange(per_level):
        first = swap(per_level[0], "seq", 1)
        across = []
        for m in range(1, nz):
            across.append((m.bit_length(), swap(per_level[m.bit_length()], "seq", 2 * m)))
        got = [[first]] + [[] for _ in range(upper - 1)]
        for at, x in across:
            got[at] += [x, swap(x, "seq", 1)]
        axis = per_level[0].ndim - 2
        return [x if x[0].shape[axis] >= 16 else [jnp.concatenate(x, axis=axis)] for x in got]

    pairs = exchange(own)
    pieces = [len(x) for x in pairs]
    flat = [x for part in pairs for x in part]

    grads = [g] + [swap(g, "dp", m) for m in range(1, min(dp, 3))]
    if dp == 4:
        half = tokens // 2
        grads.append(
            (swap(grads[1][:half], "dp", 2), swap(grads[2][half:], "dp", 1))
        )
    else:
        grads += [swap(g, "dp", m) for m in range(3, dp)]

    early = call(
        functools.partial(early_kernel, levels),
        [((upper, tokens, width), BF16), ((tokens, width), BF16)]
        + [((tokens >> l, width), BF16) for l in range(1, levels)],
        "early",
        2 * tokens * width * width + 2 * upper * tokens * tokens * width,
        q,
        g,
        w_out,
    )
    qhat, ga, qls = early[0], early[1], early[2:]

    total_keys = tokens + upper * BLOCK
    forward = call(
        functools.partial(forward_kernel, levels, pieces, dp),
        [
            ((HEADS, tokens, total_keys), BF16),
            ((tokens, width), BF16),
            ((tokens, LANES), F32),
            ((tokens, width), BF16),
        ]
        + [((tokens, width // dp), BF16)] * dp
        + [((tokens >> l, 2 * width + LANES), BF16) for l in range(1, levels)],
        "forward",
        6 * tokens * total_keys * width,
        q,
        k,
        v,
        qhat,
        ga,
        *qls,
        *flat,
    )
    e, gr, dd, att = forward[:4]
    blocks, outgoing = forward[4 : 4 + dp], forward[4 + dp :]

    atts = [blocks[0]] + [swap(blocks[m], "dp", m) for m in range(1, dp)]
    messages = exchange(outgoing)
    message_pieces = [len(x) for x in messages]

    if dp == 4:
        grads[3] = jnp.concatenate(grads[3], axis=0)
    rows = width // dp
    keep, send = pl.pallas_call(
        functools.partial(weight_kernel, dp, nz),
        name="weight",
        out_shape=[
            jax.ShapeDtypeStruct((rows // 2, width), F32),
            jax.ShapeDtypeStruct((rows // 2, width), BF16),
        ],
        in_specs=[pl.BlockSpec(memory_space=pltpu.VMEM)] * (2 * dp),
        out_specs=[pl.BlockSpec(memory_space=pltpu.VMEM)] * 2,
        scratch_shapes=[pltpu.VMEM((rows, width), F32)],
        compiler_params=pltpu.CompilerParams(vmem_limit_bytes=VMEM_LIMIT),
        cost_estimate=pl.CostEstimate(
            flops=2 * tokens * width * width, bytes_accessed=4 << 20, transcendentals=0
        ),
    )(*atts, *grads)
    got = swap(send, "seq", 1)
    own_rows = rows // (2 * nz)
    parts = call(
        halves_kernel,
        [((own_rows, width), F32)] + [((own_rows, width), BF16)] * (nz - 1),
        "halves",
        rows * width,
        keep,
        got,
    )
    parts = [parts[0]] + [swap(parts[m], "seq", 2 * m) for m in range(1, nz)]

    gq, dk0, dv0, mixed = pl.pallas_call(
        functools.partial(backward_kernel, levels, pieces),
        name="backward",
        out_shape=[
            jax.ShapeDtypeStruct((tokens, width), F32),
            jax.ShapeDtypeStruct((tokens, width), BF16),
            jax.ShapeDtypeStruct((tokens, width), BF16),
            jax.ShapeDtypeStruct((tokens, width), BF16),
        ],
        in_specs=[pl.BlockSpec(memory_space=pltpu.VMEM)] * (9 + len(flat)),
        out_specs=[pl.BlockSpec(memory_space=pltpu.VMEM)] * 4,
        scratch_shapes=[pltpu.VMEM((upper * tokens, width), BF16)],
        compiler_params=pltpu.CompilerParams(vmem_limit_bytes=VMEM_LIMIT),
        cost_estimate=pl.CostEstimate(
            flops=10 * tokens * total_keys * width, bytes_accessed=8 << 20, transcendentals=0
        ),
    )(e, gr, dd, ga, q, k, v, *flat, att, w_out)

    upper_rows = sum(tokens >> l for l in range(1, levels))
    flat_messages = [x for part in messages for x in part]
    gk, gv = pl.pallas_call(
        functools.partial(owner_kernel, levels, message_pieces, tokens),
        name="owner",
        out_shape=[jax.ShapeDtypeStruct((tokens, width), BF16)] * 2,
        in_specs=[pl.BlockSpec(memory_space=pltpu.VMEM)] * (upper + len(flat_messages) + 2),
        out_specs=[pl.BlockSpec(memory_space=pltpu.VMEM)] * 2,
        scratch_shapes=[pltpu.VMEM((upper_rows, width), BF16)] * 2,
        compiler_params=pltpu.CompilerParams(vmem_limit_bytes=VMEM_LIMIT),
        cost_estimate=pl.CostEstimate(
            flops=8 * BLOCK * upper_rows * width, bytes_accessed=5 << 20, transcendentals=0
        ),
    )(*own, *flat_messages, dk0, dv0)

    (gw,) = call(
        functools.partial(final_kernel, factor),
        [((own_rows, width), F32)],
        "total",
        rows * width,
        *parts,
    )
    return (mixed[None], gq.astype(BF16)[None], gk[None], gv[None], gw)


def solution(mesh):
    rows = P("dp", "seq", None)
    return jax.shard_map(
        body,
        mesh=mesh,
        in_specs=(rows, rows, rows, rows, P()),
        out_specs=(rows, rows, rows, rows, P(("dp", "seq"), None)),
        check_vma=False,
    )
```

```python
import functools
import math

import jax
import jax.numpy as jnp
from jax import lax
from jax.experimental import pallas as pl
from jax.experimental.pallas import tpu as pltpu
from jax.sharding import PartitionSpec as P

HEADS = 8
HEAD_DIM = 128
BLOCK = 128
LANES = 128
SCALE = 1.0 / math.sqrt(HEAD_DIM)
SCALE2 = SCALE / math.log(2.0)
F32 = jnp.float32
BF16 = jnp.bfloat16
COST = 5_000_000_000
VMEM_LIMIT = 24 * 1024 * 1024


def dot(a, b, dims):
    return lax.dot_general(a, b, (dims, ((), ())), preferred_element_type=F32)


def nn(a, b):
    return dot(a, b, ((1,), (0,)))


def nt(a, b):
    return dot(a, b, ((1,), (1,)))


def tn(a, b):
    return dot(a, b, ((0,), (0,)))


def member(rows, cols, row_shift, col_shift, value):
    r = lax.broadcasted_iota(jnp.int32, (rows, cols), 0) >> row_shift
    c = lax.broadcasted_iota(jnp.int32, (rows, cols), 1) >> col_shift
    return jnp.where(r == c, value, 0.0).astype(BF16)


def call(kernel, outs, name, cost, *operands, scratch=(), space=pltpu.VMEM):
    return pl.pallas_call(
        kernel,
        name=name,
        out_shape=[jax.ShapeDtypeStruct(s, t) for s, t in outs],
        in_specs=[pl.BlockSpec(memory_space=space)] * len(operands),
        out_specs=[pl.BlockSpec(memory_space=pltpu.VMEM)] * len(outs),
        scratch_shapes=list(scratch),
        compiler_params=pltpu.CompilerParams(vmem_limit_bytes=VMEM_LIMIT),
        cost_estimate=pl.CostEstimate(flops=cost, bytes_accessed=1, transcendentals=0),
    )(*operands)


def pool_kernel(levels, k_ref, v_ref, *refs):
    outs, (held, sems) = refs[:-2], refs[-2:]
    tokens, width = k_ref.shape
    copies = [
        pltpu.make_async_copy(src, held.at[i], sems.at[i]) for i, src in enumerate((k_ref, v_ref))
    ]
    for copy in copies:
        copy.start()
    pools = [member(tokens >> l, tokens, 0, l, 0.5**l) for l in range(1, levels)]
    for i, copy in enumerate(copies):
        copy.wait()
        for pool, out in zip(pools, outs):
            out[i] = nn(pool, held[i]).astype(BF16)


def early_kernel(levels, q_ref, g_ref, w_ref, qhat_ref, gat_ref, *qls):
    tokens, width = q_ref.shape
    q = q_ref[...]
    for l in range(1, levels):
        qhat_ref[l - 1] = nn(member(tokens, tokens, l, l, 0.5**l), q).astype(BF16)
        qls[l - 1][...] = nn(member(tokens >> l, tokens, 0, l, 0.5**l), q).astype(BF16)
    g = g_ref[...]
    for c in range(0, width, 256):
        gat_ref[c : c + 256, :] = nt(w_ref[c : c + 256, :], g).astype(BF16)


def gathered(levels, pieces, kvs, which, hs):
    out, at = [], 0
    for l in range(1, levels):
        part = kvs[at : at + pieces[l - 1]]
        at += pieces[l - 1]
        out.append(jnp.concatenate([p[which, :, hs] for p in part], axis=0))
    return out


def forward_kernel(levels, pieces, dp, q_ref, k_ref, v_ref, qhat_ref, gat_ref, *refs):
    tokens, width = q_ref.shape
    upper = levels - 1
    count = sum(pieces)
    qls, refs = refs[:upper], refs[upper:]
    kvs, refs = refs[:count], refs[count:]
    e_ref, grt_ref, dd_ref, att_ref = refs[:4]
    blocks, msgs, aux_ref = refs[4 : 4 + dp], refs[4 + dp : -1], refs[-1]
    ones = jnp.ones((16, tokens + upper * BLOCK), BF16)
    sums = [member(tokens >> l, tokens, 0, l, 1.0) for l in range(1, levels)]
    aux_ref[...] = jnp.zeros_like(aux_ref)

    def scores(h):
        hs = slice(h * HEAD_DIM, (h + 1) * HEAD_DIM)
        keys = gathered(levels, pieces, kvs, 0, hs)
        return [nt(k_ref[:, hs], q_ref[:, hs])] + [
            nt(keys[l - 1], qhat_ref[l - 1, :, hs]) for l in range(1, levels)
        ]

    def attend(h, raws):
        hs = slice(h * HEAD_DIM, (h + 1) * HEAD_DIM)
        tops = [jnp.max(raw, axis=0, keepdims=True) for raw in raws]
        top = tops[0] * SCALE2
        for l in range(1, levels):
            top = jnp.maximum(top, tops[l] * SCALE2 + float(l))
        at, es = 0, []
        for l, raw in enumerate(raws):
            es.append(jnp.exp2(raw * SCALE2 + (float(l) - top)).astype(BF16))
            e_ref[h, at : at + raw.shape[0], :] = es[-1]
            at += raw.shape[0]
        vals = jnp.concatenate([v_ref[:, hs]] + gathered(levels, pieces, kvs, 1, hs), axis=0)
        lhs = jnp.concatenate([vals.T, ones], axis=0)
        return top, tops, nn(lhs, jnp.concatenate(es, axis=0))

    def finish(h, top, tops, both):
        hs = slice(h * HEAD_DIM, (h + 1) * HEAD_DIM)
        rden = 1.0 / both[HEAD_DIM : HEAD_DIM + 1]
        att = (both[:HEAD_DIM] * rden).astype(BF16)
        att_ref[hs, :] = att
        grt = gat_ref[hs, :].astype(F32) * rden
        grt_ref[hs, :] = grt.astype(BF16)
        delta = jnp.sum(grt * att.astype(F32), axis=0, keepdims=True)
        dd_ref[h : h + 1, :] = delta
        for l in range(1, levels):
            mu = tops[l].astype(BF16).astype(F32)
            a = jnp.exp2(mu * SCALE2 + (float(l) - top))
            msgs[l - 1][:, hs] = nt(sums[l - 1], (grt * a).astype(BF16)).astype(BF16)
            aux_ref[l - 1, h : h + 1, :] = mu * 0.5**l
            aux_ref[l - 1, HEADS + h : HEADS + h + 1, :] = delta * a

    ahead, behind = scores(0), None
    for h in range(HEADS):
        raws = ahead
        if h + 1 < HEADS:
            ahead = scores(h + 1)
        state = attend(h, raws)
        if behind is not None:
            finish(h - 1, *behind)
        behind = state
    finish(HEADS - 1, *behind)
    me = lax.axis_index("dp")
    span = width // dp
    for m in range(dp):
        at = pl.multiple_of((me ^ m) * span, span)
        blocks[m][...] = att_ref[pl.ds(at, span), :]
    for l in range(1, levels):
        msgs[l - 1][:, width : 2 * width] = qls[l - 1][...]
        msgs[l - 1][:, 2 * width :] = nt(sums[l - 1], aux_ref[l - 1].astype(BF16)).astype(BF16)


def backward_kernel(levels, pieces, e_ref, grt_ref, dd_ref, q_ref, k_ref, v_ref, *refs):
    tokens, width = q_ref.shape
    count = sum(pieces)
    kvs = refs[:count]
    gq_ref, dk_ref, dv_ref, y_ref = refs[count:]
    starts = [0] + [tokens + l * BLOCK for l in range(levels)]

    def probs(h):
        hs = slice(h * HEAD_DIM, (h + 1) * HEAD_DIM)
        vals = jnp.concatenate([v_ref[:, hs]] + gathered(levels, pieces, kvs, 1, hs), axis=0)
        return nn(vals, grt_ref[hs, :])

    def rest(h, dpt):
        hs = slice(h * HEAD_DIM, (h + 1) * HEAD_DIM)
        e = e_ref[h]
        ds = (e.astype(F32) * (dpt - dd_ref[h : h + 1, :])).astype(BF16)
        keys = [k_ref[:, hs]] + gathered(levels, pieces, kvs, 0, hs)
        for l in range(levels):
            part = ds[starts[l] : starts[l + 1]]
            y_ref[hs, l * tokens : (l + 1) * tokens] = tn(keys[l], part).astype(BF16)
        dv_ref[:, hs] = nt(e[:tokens], grt_ref[hs, :]).astype(BF16)
        dk_ref[:, hs] = (nn(ds[:tokens], q_ref[:, hs]) * SCALE).astype(BF16)

    ahead = probs(0)
    for h in range(HEADS):
        dpt = ahead
        if h + 1 < HEADS:
            ahead = probs(h + 1)
        rest(h, dpt)
    spread = jnp.concatenate(
        [member(tokens, tokens, l, l, 0.5**l) for l in range(levels)], axis=1
    )
    for c in range(0, width, 256):
        cs = slice(c, c + 256)
        gq_ref[:, cs] = (nt(spread, y_ref[cs, :]) * SCALE).astype(BF16)


def weight_kernel(dp, nz, *refs):
    atts, refs = refs[:dp], refs[dp:]
    grads, (keep_ref, even_ref, odd_ref, total_ref) = refs[:-4], refs[-4:]
    a = jnp.concatenate([x[...] for x in atts], axis=1)
    width = grads[0].shape[1]
    for c in range(0, width, 256):
        cs = slice(c, c + 256)
        g = jnp.concatenate([x[:, cs] for x in grads], axis=0)
        total_ref[:, cs] = nn(a, g)
    rows = total_ref.shape[0] // (2 * nz)
    seq = lax.axis_index("seq")
    core, z = seq & 1, seq >> 1
    for m in range(nz):
        base = (z ^ m) * 2 * rows
        mine = pl.multiple_of(base + core * rows, rows)
        other = pl.multiple_of(base + (1 - core) * rows, rows)
        keep_ref[m] = total_ref[pl.ds(mine, rows), :]
        send_ref = odd_ref if m % 2 else even_ref
        send_ref[m // 2] = total_ref[pl.ds(other, rows), :].astype(BF16)


def halve_kernel(offset, count, keep_ref, *refs):
    got, relay, (next_ref, send_ref) = refs[:count], refs[count:-2], refs[-2:]
    width = keep_ref.shape[2]

    def total(i):
        if offset is None:
            came = got[i % 2][i // 2]
        else:
            came = got[0][:, offset + i * width : offset + (i + 1) * width]
        return keep_ref[i] + came.astype(F32)

    for i in range(next_ref.shape[0]):
        next_ref[i] = total(2 * i)
        out = total(2 * i + 1).astype(BF16)
        if relay:
            at = relay[0].shape[1] + i * width
            send_ref[:, at : at + width] = out
        else:
            send_ref[i] = out
    if relay:
        send_ref[:, : relay[0].shape[1]] = relay[0][...]


def mixed_kernel(att_ref, w_ref, out_ref):
    att = att_ref[...].T
    for c in range(0, w_ref.shape[1], 256):
        out_ref[:, c : c + 256] = nn(att, w_ref[:, c : c + 256]).astype(BF16)


def final_kernel(factor, keep_ref, got_ref, out_ref):
    out_ref[...] = (keep_ref[0] + got_ref[0].astype(F32)) * factor


def owner_kernel(levels, pieces, tokens, *refs):
    upper = levels - 1
    count = sum(pieces)
    kvs, refs = refs[:upper], refs[upper:]
    msgs, refs = refs[:count], refs[count:]
    dk0_ref, dv0_ref, gk_ref, gv_ref, dks_ref, dvs_ref = refs
    width = dk0_ref.shape[1]
    auxes, at = [], 0
    groups = []
    for l in range(1, levels):
        part = msgs[at : at + pieces[l - 1]]
        at += pieces[l - 1]
        groups.append(part)
        auxes.append(jnp.concatenate([p[:, 2 * width : 2 * width + LANES] for p in part], axis=0))
    lane = lax.broadcasted_iota(jnp.int32, (tokens >> 1, LANES), 1)

    def products(h):
        hs = slice(h * HEAD_DIM, (h + 1) * HEAD_DIM)
        qs = slice(width + h * HEAD_DIM, width + (h + 1) * HEAD_DIM)
        minus_mu = jnp.where(lane == h, -1.0, 0.0).astype(BF16)
        minus_d = jnp.where(lane == HEADS + h, -1.0, 0.0).astype(BF16)
        out = []
        for l in range(1, levels):
            n = tokens >> l
            ga = jnp.concatenate([p[:, hs] for p in groups[l - 1]], axis=0)
            q = jnp.concatenate([p[:, qs] for p in groups[l - 1]], axis=0)
            aux = auxes[l - 1]
            k = jnp.concatenate([kvs[l - 1][0, :, hs], minus_mu[:n]], axis=1)
            v = jnp.concatenate([kvs[l - 1][1, :, hs], minus_d[:n]], axis=1)
            raw = nt(k, jnp.concatenate([q, aux], axis=1))
            out.append((ga, q, raw, nt(v, jnp.concatenate([ga, aux], axis=1))))
        return out

    def gradients(h, parts):
        hs = slice(h * HEAD_DIM, (h + 1) * HEAD_DIM)
        at = 0
        for ga, q, raw, dp_raw in parts:
            n = raw.shape[0]
            e = jnp.exp2(raw * SCALE2)
            ds = (e * dp_raw).astype(BF16)
            dvs_ref[at : at + n, hs] = nn(e.astype(BF16), ga).astype(BF16)
            dks_ref[at : at + n, hs] = (nn(ds, q) * SCALE).astype(BF16)
            at += n

    ahead = products(0)
    for h in range(HEADS):
        parts = ahead
        if h + 1 < HEADS:
            ahead = products(h + 1)
        gradients(h, parts)
    total = dks_ref.shape[0]
    spread = jnp.concatenate(
        [member(tokens, tokens >> l, l, 0, 0.5**l) for l in range(1, levels)], axis=1
    )
    for c in range(0, width, 256):
        cs = slice(c, c + 256)
        gk_ref[:, cs] = (dk0_ref[:, cs].astype(F32) + nn(spread, dks_ref[:, cs])).astype(BF16)
        gv_ref[:, cs] = (dv0_ref[:, cs].astype(F32) + nn(spread, dvs_ref[:, cs])).astype(BF16)


def after(x, *others):
    return lax.optimization_barrier((x, *others))[0]


def swap(x, axis, mask):
    count = lax.axis_size(axis)
    return lax.ppermute(x, axis, [(i, i ^ mask) for i in range(count)])


def body(queries, keys, values, grad_out, w_out):
    seq = lax.axis_size("seq")
    dp = lax.axis_size("dp")
    nz = seq // 2
    levels = seq.bit_length()
    upper = levels - 1
    q, k, v, g = queries[0], keys[0], values[0], grad_out[0]
    tokens, width = q.shape
    factor = 1.0 / math.sqrt(dp * seq * tokens)

    own = call(
        functools.partial(pool_kernel, levels),
        [((2, tokens >> l, width), BF16) for l in range(1, levels)],
        "pool",
        1,
        k,
        v,
        scratch=[pltpu.VMEM((2, tokens, width), BF16), pltpu.SemaphoreType.DMA((2,))],
        space=pltpu.HBM,
    )

    def across(per_level):
        return [
            (m.bit_length(), swap(per_level[m.bit_length()], "seq", 2 * m)) for m in range(1, nz)
        ]

    def joined(first, received, *wait):
        got = [[swap(first, "seq", 1)]] + [[] for _ in range(upper - 1)]
        for at, x in received:
            x = after(x, *wait)
            got[at] += [x, swap(x, "seq", 1)]
        axis = first.ndim - 2
        return [x if x[0].shape[axis] >= 16 else [jnp.concatenate(x, axis=axis)] for x in got]

    received = across(own)

    early = call(
        functools.partial(early_kernel, levels),
        [((upper, tokens, width), BF16), ((width, tokens), BF16)]
        + [((tokens >> l, width), BF16) for l in range(1, levels)],
        "early",
        1,
        after(q, own[0]),
        g,
        w_out,
    )
    qhat, gat, qls = early[0], early[1], early[2:]

    g_late = g
    grads = [g] + [swap(g_late, "dp", m) for m in range(1, min(dp, 3))]
    if dp == 4:
        half = tokens // 2
        grads += [swap(grads[1][:half], "dp", 2), swap(grads[2][half:], "dp", 1)]
    else:
        grads += [swap(g_late, "dp", m) for m in range(3, dp)]

    arrived = [x for _, x in received]
    pairs = joined(after(own[0], *arrived, gat), received, *arrived, gat)
    pieces = [len(x) for x in pairs]
    flat = [x for part in pairs for x in part]

    total_keys = tokens + upper * BLOCK
    outs = [
        ((HEADS, total_keys, tokens), BF16),
        ((width, tokens), BF16),
        ((HEADS, tokens), F32),
        ((width, tokens), BF16),
    ]
    outs += [((width // dp, tokens), BF16)] * dp
    outs += [((tokens >> l, 2 * width + LANES), BF16) for l in range(1, levels)]
    forward = call(
        functools.partial(forward_kernel, levels, pieces, dp),
        outs,
        "forward",
        1,
        q,
        k,
        v,
        qhat,
        gat,
        *qls,
        *flat,
        scratch=[pltpu.VMEM((upper, LANES, tokens), F32)],
    )
    e, grt, dd, att = forward[:4]
    blocks, outgoing = forward[4 : 4 + dp], forward[4 + dp :]

    atts = [blocks[0]] + [swap(blocks[m], "dp", m) for m in range(1, dp)]
    outgoing = list(lax.optimization_barrier((*outgoing, *grads[3:]))[:upper])
    relayed = nz == 4
    if relayed:
        far = swap(outgoing[2], "seq", 4)
        near = swap(outgoing[1], "seq", 2)
    else:
        received = across(outgoing)

    rows = width // dp
    own_rows = rows // (2 * nz)
    keep, even, odd = call(
        functools.partial(weight_kernel, dp, nz),
        [((nz, own_rows, width), F32)] + [((nz // 2, own_rows, width), BF16)] * 2,
        "weight",
        COST,
        *atts,
        *grads,
        scratch=[pltpu.VMEM((rows, width), F32)],
    )

    def halve(keep, got, offset=None, relay=()):
        n = keep.shape[0] // 2
        sent = (n, own_rows, width)
        if relay:
            sent = (own_rows, relay[0].shape[1] + n * width)
        outs = [((n, own_rows, width), F32), (sent, BF16)]
        kernel = functools.partial(halve_kernel, offset, len(got))
        return call(kernel, outs, "halve", 1, keep, *got, *relay)

    got = [swap(even, "seq", 1), swap(odd, "seq", 1)]
    if relayed:
        keep, send = halve(keep, got, None, (far,))
        both = swap(send, "seq", 2)
        grt = after(grt, keep, near)
    else:
        keep, send = halve(keep, got)
        grt = after(grt, keep)

    gq, dk0, dv0 = call(
        functools.partial(backward_kernel, levels, pieces),
        [((tokens, width), BF16)] * 3,
        "backward",
        COST,
        e,
        grt,
        dd,
        q,
        k,
        v,
        *flat,
        scratch=[pltpu.VMEM((width, levels * tokens), BF16)],
    )

    keep = after(keep, dk0)
    if relayed:
        keep, send = halve(keep, [both], far.shape[1])
        step = 4
        first = swap(after(outgoing[0], got[0]), "seq", 1)
        near, far, both = (after(x, dk0, send) for x in (near, far, both))
        messages = [
            [first],
            [near, swap(near, "seq", 1)],
            [far, swap(far, "seq", 1), both, swap(both, "seq", 1)],
        ]
    else:
        step = 2
        while keep.shape[0] > 1:
            got = swap(send, "seq", step)
            keep, send = halve(keep, [got[0::2], got[1::2]])
            step *= 2
        messages = joined(after(outgoing[0], dk0, send), received, dk0, send)
    message_pieces = [len(x) for x in messages]
    flat_messages = [x for part in messages for x in part]

    (mixed,) = call(
        mixed_kernel, [((tokens, width), BF16)], "mixed", 1, after(att, send), w_out
    )
    upper_rows = sum(tokens >> l for l in range(1, levels))
    gk, gv = call(
        functools.partial(owner_kernel, levels, message_pieces, tokens),
        [((tokens, width), BF16)] * 2,
        "owner",
        1,
        *own,
        *flat_messages,
        dk0,
        dv0,
        scratch=[pltpu.VMEM((upper_rows, width), BF16)] * 2,
    )

    (gw,) = call(
        functools.partial(final_kernel, factor),
        [((own_rows, width), F32)],
        "total",
        1,
        after(keep, gk),
        swap(send, "seq", step),
    )
    return (mixed[None], gq[None], gk[None], gv[None], gw)


def solution(mesh):
    rows = P("dp", "seq", None)
    return jax.shard_map(
        body,
        mesh=mesh,
        in_specs=(rows, rows, rows, rows, P()),
        out_specs=(rows, rows, rows, rows, P(("dp", "seq"), None)),
        check_vma=False,
    )
```

```python
import functools
import math

import jax
import jax.numpy as jnp
from jax import lax
from jax.experimental import pallas as pl
from jax.experimental.pallas import tpu as pltpu
from jax.sharding import PartitionSpec as P

HEADS = 8
HEAD_DIM = 128
BLOCK = 128
LANES = 128
SCALE = 1.0 / math.sqrt(HEAD_DIM)
SCALE2 = SCALE / math.log(2.0)
F32 = jnp.float32
BF16 = jnp.bfloat16
COST = 5_000_000_000
VMEM_LIMIT = 24 * 1024 * 1024


def dot(a, b, dims):
    return lax.dot_general(a, b, (dims, ((), ())), preferred_element_type=F32)


def nn(a, b):
    return dot(a, b, ((1,), (0,)))


def nt(a, b):
    return dot(a, b, ((1,), (1,)))


def tn(a, b):
    return dot(a, b, ((0,), (0,)))


def member(rows, cols, row_shift, col_shift, value):
    r = lax.broadcasted_iota(jnp.int32, (rows, cols), 0) >> row_shift
    c = lax.broadcasted_iota(jnp.int32, (rows, cols), 1) >> col_shift
    return jnp.where(r == c, value, 0.0).astype(BF16)


def call(kernel, outs, name, cost, *operands, scratch=(), space=pltpu.VMEM):
    return pl.pallas_call(
        kernel,
        name=name,
        out_shape=[jax.ShapeDtypeStruct(s, t) for s, t in outs],
        in_specs=[pl.BlockSpec(memory_space=space)] * len(operands),
        out_specs=[pl.BlockSpec(memory_space=pltpu.VMEM)] * len(outs),
        scratch_shapes=list(scratch),
        compiler_params=pltpu.CompilerParams(vmem_limit_bytes=VMEM_LIMIT),
        cost_estimate=pl.CostEstimate(flops=cost, bytes_accessed=1, transcendentals=0),
    )(*operands)


def pool_kernel(levels, k_ref, v_ref, *refs):
    outs, (held, sems) = refs[:-2], refs[-2:]
    tokens, width = k_ref.shape
    copies = [
        pltpu.make_async_copy(src, held.at[i], sems.at[i]) for i, src in enumerate((k_ref, v_ref))
    ]
    for copy in copies:
        copy.start()
    pools = [member(tokens >> l, tokens, 0, l, 0.5**l) for l in range(1, levels)]
    for i, copy in enumerate(copies):
        copy.wait()
        for pool, out in zip(pools, outs):
            out[i] = nn(pool, held[i]).astype(BF16)


def early_kernel(levels, q_ref, k_ref, v_ref, g_ref, w_ref, *refs):
    qhat_ref, gat_ref, e_ref, o_ref, stat_ref = refs[:5]
    qls = refs[5:]
    tokens, width = q_ref.shape
    q = q_ref[...]
    for l in range(1, levels):
        qhat_ref[l - 1] = nn(member(tokens, tokens, l, l, 0.5**l), q).astype(BF16)
        qls[l - 1][...] = nn(member(tokens >> l, tokens, 0, l, 0.5**l), q).astype(BF16)
    ones = jnp.ones((16, tokens), BF16)

    def attend(h, raw):
        hs = slice(h * HEAD_DIM, (h + 1) * HEAD_DIM)
        top = jnp.max(raw, axis=0, keepdims=True) * SCALE2
        e = jnp.exp2(raw * SCALE2 - top).astype(BF16)
        e_ref[h] = e
        both = nn(jnp.concatenate([v_ref[:, hs].T, ones], axis=0), e)
        o_ref[hs, :] = both[:HEAD_DIM]
        stat_ref[h : h + 1, :] = top
        stat_ref[HEADS + h : HEADS + h + 1, :] = both[HEAD_DIM : HEAD_DIM + 1]

    def scores(h):
        hs = slice(h * HEAD_DIM, (h + 1) * HEAD_DIM)
        return nt(k_ref[:, hs], q_ref[:, hs])

    g = g_ref[...]
    ahead = scores(0)
    for h in range(HEADS):
        raw = ahead
        if h + 1 < HEADS:
            ahead = scores(h + 1)
        if h % 2 == 0:
            rows = slice(h * HEAD_DIM, (h + 2) * HEAD_DIM)
            gat_ref[rows, :] = nt(w_ref[rows, :], g).astype(BF16)
        attend(h, raw)


def gathered(levels, pieces, kvs, which, hs):
    out, at = [], 0
    for l in range(1, levels):
        part = kvs[at : at + pieces[l - 1]]
        at += pieces[l - 1]
        out.append(jnp.concatenate([p[which, :, hs] for p in part], axis=0))
    return out


def forward_kernel(levels, pieces, dp, qhat_ref, gat_ref, o_ref, stat_ref, *refs):
    width, tokens = gat_ref.shape
    upper = levels - 1
    count = sum(pieces)
    qls, refs = refs[:upper], refs[upper:]
    kvs, refs = refs[:count], refs[count:]
    e_ref, grt_ref, grt0_ref, dd_ref, att_ref = refs[:5]
    blocks, msgs, aux_ref = refs[5 : 5 + dp], refs[5 + dp : -1], refs[-1]
    ones = jnp.ones((16, upper * BLOCK), BF16)
    sums = [member(tokens >> l, tokens, 0, l, 1.0) for l in range(1, levels)]
    aux_ref[...] = jnp.zeros_like(aux_ref)

    def scores(h):
        hs = slice(h * HEAD_DIM, (h + 1) * HEAD_DIM)
        keys = gathered(levels, pieces, kvs, 0, hs)
        return [nt(keys[l - 1], qhat_ref[l - 1, :, hs]) for l in range(1, levels)]

    def attend(h, raws):
        hs = slice(h * HEAD_DIM, (h + 1) * HEAD_DIM)
        tops = [jnp.max(raw, axis=0, keepdims=True) for raw in raws]
        top = stat_ref[h : h + 1, :]
        for l in range(1, levels):
            top = jnp.maximum(top, tops[l - 1] * SCALE2 + float(l))
        es = []
        for l, raw in enumerate(raws, 1):
            es.append(jnp.exp2(raw * SCALE2 + (float(l) - top)).astype(BF16))
            e_ref[h, (l - 1) * BLOCK : l * BLOCK, :] = es[-1]
        vals = jnp.concatenate(gathered(levels, pieces, kvs, 1, hs), axis=0)
        lhs = jnp.concatenate([vals.T, ones], axis=0)
        return top, tops, nn(lhs, jnp.concatenate(es, axis=0))

    def finish(h, top, tops, both):
        hs = slice(h * HEAD_DIM, (h + 1) * HEAD_DIM)
        a0 = jnp.exp2(stat_ref[h : h + 1, :] - top)
        den0 = stat_ref[HEADS + h : HEADS + h + 1, :]
        rden = 1.0 / (both[HEAD_DIM : HEAD_DIM + 1] + den0 * a0)
        att = ((both[:HEAD_DIM] + o_ref[hs, :] * a0) * rden).astype(BF16)
        att_ref[hs, :] = att
        grt = gat_ref[hs, :].astype(F32) * rden
        grt_ref[hs, :] = grt.astype(BF16)
        grt0_ref[hs, :] = (grt * a0).astype(BF16)
        delta = jnp.sum(grt * att.astype(F32), axis=0, keepdims=True)
        dd_ref[h : h + 1, :] = delta
        dd_ref[HEADS + h : HEADS + h + 1, :] = delta * a0
        for l in range(1, levels):
            mu = tops[l - 1].astype(BF16).astype(F32)
            a = jnp.exp2(mu * SCALE2 + (float(l) - top))
            msgs[l - 1][:, hs] = nt(sums[l - 1], (grt * a).astype(BF16)).astype(BF16)
            aux_ref[l - 1, h : h + 1, :] = mu * 0.5**l
            aux_ref[l - 1, HEADS + h : HEADS + h + 1, :] = delta * a

    ahead, behind = scores(0), None
    for h in range(HEADS):
        raws = ahead
        if h + 1 < HEADS:
            ahead = scores(h + 1)
        state = attend(h, raws)
        if behind is not None:
            finish(h - 1, *behind)
        behind = state
    finish(HEADS - 1, *behind)
    me, core = lax.axis_index("dp"), lax.axis_index("seq") & 1
    span = width // dp
    for role in range(dp):
        at = pl.multiple_of((me ^ role_mask(role, core, dp)) * span, span)
        blocks[role][...] = att_ref[pl.ds(at, span), :]
    for l in range(1, levels):
        msgs[l - 1][:, width : 2 * width] = qls[l - 1][...]
        msgs[l - 1][:, 2 * width :] = nt(sums[l - 1], aux_ref[l - 1].astype(BF16)).astype(BF16)


def backward_kernel(levels, pieces, e0_ref, e_ref, grt0_ref, grt_ref, dd_ref, *refs):
    q_ref, k_ref, v_ref = refs[:3]
    tokens, width = q_ref.shape
    kvs, (gq_ref, dk_ref, dv_ref, y_ref) = refs[3:-4], refs[-4:]

    def probs(h):
        hs = slice(h * HEAD_DIM, (h + 1) * HEAD_DIM)
        vals = jnp.concatenate(gathered(levels, pieces, kvs, 1, hs), axis=0)
        return nn(v_ref[:, hs], grt0_ref[hs, :]), nn(vals, grt_ref[hs, :])

    def rest(h, dpt0, dpt):
        hs = slice(h * HEAD_DIM, (h + 1) * HEAD_DIM)
        e0 = e0_ref[h]
        ds0 = (e0.astype(F32) * (dpt0 - dd_ref[HEADS + h : HEADS + h + 1, :])).astype(BF16)
        ds = (e_ref[h].astype(F32) * (dpt - dd_ref[h : h + 1, :])).astype(BF16)
        keys = gathered(levels, pieces, kvs, 0, hs)
        y_ref[hs, :tokens] = tn(k_ref[:, hs], ds0).astype(BF16)
        for l in range(1, levels):
            part = ds[(l - 1) * BLOCK : l * BLOCK]
            y_ref[hs, l * tokens : (l + 1) * tokens] = tn(keys[l - 1], part).astype(BF16)
        dv_ref[:, hs] = nt(e0, grt0_ref[hs, :]).astype(BF16)
        dk_ref[:, hs] = (nn(ds0, q_ref[:, hs]) * SCALE).astype(BF16)

    ahead = probs(0)
    for h in range(HEADS):
        now = ahead
        if h + 1 < HEADS:
            ahead = probs(h + 1)
        rest(h, *now)
    spread = jnp.concatenate(
        [member(tokens, tokens, l, l, 0.5**l) for l in range(levels)], axis=1
    )
    for c in range(0, width, 256):
        cs = slice(c, c + 256)
        gq_ref[:, cs] = (nt(spread, y_ref[cs, :]) * SCALE).astype(BF16)


def weight_kernel(dp, nz, *refs):
    atts, refs = refs[:dp], refs[dp:]
    grads, (keep_ref, even_ref, odd_ref, total_ref) = refs[:-4], refs[-4:]
    a = jnp.concatenate([x[...] for x in atts], axis=1)
    width = grads[0].shape[1]
    for c in range(0, width, 256):
        cs = slice(c, c + 256)
        g = jnp.concatenate([x[:, cs] for x in grads], axis=0)
        total_ref[:, cs] = nn(a, g)
    rows = total_ref.shape[0] // (2 * nz)
    seq = lax.axis_index("seq")
    core, z = seq & 1, seq >> 1
    for m in range(nz):
        base = (z ^ m) * 2 * rows
        mine = pl.multiple_of(base + core * rows, rows)
        other = pl.multiple_of(base + (1 - core) * rows, rows)
        keep_ref[m] = total_ref[pl.ds(mine, rows), :]
        send_ref = odd_ref if m % 2 else even_ref
        send_ref[m // 2] = total_ref[pl.ds(other, rows), :].astype(BF16)


def halve_kernel(count, keep_ref, *refs):
    got, (next_ref, send_ref) = refs[:count], refs[count:]

    def total(i):
        return keep_ref[i] + got[i % count][i // count].astype(F32)

    for i in range(next_ref.shape[0]):
        next_ref[i] = total(2 * i)
        send_ref[i] = total(2 * i + 1).astype(BF16)


def mixed_kernel(att_ref, w_ref, out_ref):
    att = att_ref[...].T
    for c in range(0, w_ref.shape[1], 256):
        out_ref[:, c : c + 256] = nn(att, w_ref[:, c : c + 256]).astype(BF16)


def final_kernel(factor, keep_ref, got_ref, out_ref):
    out_ref[...] = (keep_ref[0] + got_ref[0].astype(F32)) * factor


def owner_kernel(chosen, pieces, tokens, *refs):
    kvs, refs = refs[: len(chosen)], refs[len(chosen) :]
    msgs, refs = refs[: sum(pieces)], refs[sum(pieces) :]
    dk0_ref, dv0_ref, gk_ref, gv_ref, dks_ref, dvs_ref = refs
    width = dk0_ref.shape[1]
    auxes, at = [], 0
    groups = []
    for count in pieces:
        part = msgs[at : at + count]
        at += count
        groups.append(part)
        auxes.append(
            jnp.concatenate([p[:, 2 * width : 2 * width + LANES] for p in part], axis=0)
        )
    lane = lax.broadcasted_iota(jnp.int32, (tokens >> 1, LANES), 1)

    def products(h):
        hs = slice(h * HEAD_DIM, (h + 1) * HEAD_DIM)
        qs = slice(width + h * HEAD_DIM, width + (h + 1) * HEAD_DIM)
        minus_mu = jnp.where(lane == h, -1.0, 0.0).astype(BF16)
        minus_d = jnp.where(lane == HEADS + h, -1.0, 0.0).astype(BF16)
        out = []
        for group, aux, kv, l in zip(groups, auxes, kvs, chosen):
            n = tokens >> l
            ga = jnp.concatenate([p[:, hs] for p in group], axis=0)
            q = jnp.concatenate([p[:, qs] for p in group], axis=0)
            k = jnp.concatenate([kv[0, :, hs], minus_mu[:n]], axis=1)
            v = jnp.concatenate([kv[1, :, hs], minus_d[:n]], axis=1)
            raw = nt(k, jnp.concatenate([q, aux], axis=1))
            out.append((ga, q, raw, nt(v, jnp.concatenate([ga, aux], axis=1))))
        return out

    def gradients(h, parts):
        hs = slice(h * HEAD_DIM, (h + 1) * HEAD_DIM)
        at = 0
        for ga, q, raw, dp_raw in parts:
            n = raw.shape[0]
            e = jnp.exp2(raw * SCALE2)
            ds = (e * dp_raw).astype(BF16)
            dvs_ref[at : at + n, hs] = nn(e.astype(BF16), ga).astype(BF16)
            dks_ref[at : at + n, hs] = (nn(ds, q) * SCALE).astype(BF16)
            at += n

    depth = 2 if len(chosen) > 1 else HEADS
    ahead = [products(h) for h in range(depth)]
    for h in range(HEADS):
        parts = ahead.pop(0)
        if h + depth < HEADS:
            ahead.append(products(h + depth))
        gradients(h, parts)
    spread = jnp.concatenate([member(tokens, tokens >> l, l, 0, 0.5**l) for l in chosen], axis=1)
    for c in range(0, width, 256):
        cs = slice(c, c + 256)
        gk = dk0_ref[:, cs].astype(F32) + nn(spread, dks_ref[:, cs])
        gv = dv0_ref[:, cs].astype(F32) + nn(spread, dvs_ref[:, cs])
        gk_ref[:, cs] = gk.astype(gk_ref.dtype)
        gv_ref[:, cs] = gv.astype(gv_ref.dtype)


def after(x, *others):
    return lax.optimization_barrier((x, *others))[0]


def role_mask(role, core, dp):
    if dp != 4 or role % 3 == 0:
        return role
    return role + core if role == 1 else role - core


def exchange_role(x, role):
    dp, seq = lax.axis_size("dp"), lax.axis_size("seq")
    pairs = []
    for i in range(dp):
        for j in range(seq):
            pairs.append((i * seq + j, (i ^ role_mask(role, j & 1, dp)) * seq + j))
    return lax.ppermute(x, ("dp", "seq"), pairs)


def swap(x, axis, mask):
    count = lax.axis_size(axis)
    return lax.ppermute(x, axis, [(i, i ^ mask) for i in range(count)])


def body(queries, keys, values, grad_out, w_out):
    seq = lax.axis_size("seq")
    dp = lax.axis_size("dp")
    nz = seq // 2
    levels = seq.bit_length()
    upper = levels - 1
    q, k, v, g = queries[0], keys[0], values[0], grad_out[0]
    tokens, width = q.shape
    factor = 1.0 / math.sqrt(dp * seq * tokens)

    own = call(
        functools.partial(pool_kernel, levels),
        [((2, tokens >> l, width), BF16) for l in range(1, levels)],
        "pool",
        1,
        k,
        v,
        scratch=[pltpu.VMEM((2, tokens, width), BF16), pltpu.SemaphoreType.DMA((2,))],
        space=pltpu.HBM,
    )

    def across(per_level):
        return [
            (m.bit_length(), swap(per_level[m.bit_length()], "seq", 2 * m)) for m in range(1, nz)
        ]

    def joined(first, received, *wait):
        got = [[swap(first, "seq", 1)]] + [[] for _ in range(upper - 1)]
        for at, x in received:
            x = after(x, *wait)
            got[at] += [x, swap(x, "seq", 1)]
        axis = first.ndim - 2
        return [x if x[0].shape[axis] >= 16 else [jnp.concatenate(x, axis=axis)] for x in got]

    received = across(own)

    early = call(
        functools.partial(early_kernel, levels),
        [
            ((upper, tokens, width), BF16),
            ((width, tokens), BF16),
            ((HEADS, tokens, tokens), BF16),
            ((width, tokens), F32),
            ((2 * HEADS, tokens), F32),
        ]
        + [((tokens >> l, width), BF16) for l in range(1, levels)],
        "early",
        1,
        after(q, own[0]),
        k,
        v,
        g,
        w_out,
    )
    qhat, gat, e0, o0, stats = early[:5]
    qls = early[5:]

    g_late = after(g, own[0])
    grads = [g] + [exchange_role(g_late, r) for r in range(1, min(dp, 3))]
    if dp == 4:
        grads.append(exchange_role(grads[1], 2))
    else:
        grads += [exchange_role(g_late, r) for r in range(3, dp)]

    stats = after(stats, *grads[1:3])
    arrived = [x for _, x in received]
    arrived += [gat]
    pairs = joined(after(own[0], *arrived), received, *arrived)
    pieces = [len(x) for x in pairs]
    flat = [x for part in pairs for x in part]

    outs = [
        ((HEADS, upper * BLOCK, tokens), BF16),
        ((width, tokens), BF16),
        ((width, tokens), BF16),
        ((2 * HEADS, tokens), F32),
        ((width, tokens), BF16),
    ]
    outs += [((width // dp, tokens), BF16)] * dp
    outs += [((tokens >> l, 2 * width + LANES), BF16) for l in range(1, levels)]
    forward = call(
        functools.partial(forward_kernel, levels, pieces, dp),
        outs,
        "forward",
        1,
        qhat,
        gat,
        o0,
        stats,
        *qls,
        *flat,
        scratch=[pltpu.VMEM((upper, LANES, tokens), F32)],
    )
    e, grt, grt0, dd, att = forward[:5]
    blocks, outgoing = forward[5 : 5 + dp], forward[5 + dp :]

    atts = [blocks[0]] + [exchange_role(blocks[r], r) for r in range(1, dp)]
    relayed = nz == 4
    if relayed:
        far = swap(after(outgoing[2], *grads[3:4]), "seq", 4)
        near = swap(after(outgoing[1], *grads[3:]), "seq", 2)
    else:
        received = across(outgoing)

    rows = width // dp
    own_rows = rows // (2 * nz)
    keep, even, odd = call(
        functools.partial(weight_kernel, dp, nz),
        [((nz, own_rows, width), F32)] + [((nz // 2, own_rows, width), BF16)] * 2,
        "weight",
        COST,
        *atts,
        *grads,
        scratch=[pltpu.VMEM((rows, width), F32)],
    )

    def halve(keep, *got):
        n = keep.shape[0] // 2
        outs = [((n, own_rows, width), F32), ((n, own_rows, width), BF16)]
        return call(functools.partial(halve_kernel, len(got)), outs, "halve", 1, keep, *got)

    keep, send = halve(keep, swap(even, "seq", 1), swap(odd, "seq", 1))
    came = swap(send, "seq", 2)
    if relayed:
        relay = swap(after(far, keep, near), "seq", 2)
        near = after(near, keep)
    grt = after(grt, keep)

    gq, dk0, dv0 = call(
        functools.partial(backward_kernel, levels, pieces),
        [((tokens, width), BF16)] * 3,
        "backward",
        COST,
        e0,
        e,
        grt0,
        grt,
        dd,
        q,
        k,
        v,
        *flat,
        scratch=[pltpu.VMEM((width, levels * tokens), BF16)],
    )

    def owned(chosen, messages, dk, dv, dtype):
        flat = [x for part in messages for x in part]
        rows = sum(tokens >> l for l in chosen)
        return call(
            functools.partial(owner_kernel, chosen, [len(x) for x in messages], tokens),
            [((tokens, width), dtype)] * 2,
            "owner",
            1,
            *[own[l - 1] for l in chosen],
            *flat,
            dk,
            dv,
            scratch=[pltpu.VMEM((rows, width), BF16)] * 2,
        )

    last = levels - 1
    some = list(range(1, last))
    step = 2
    first = after(outgoing[0], keep)
    keep = after(keep, dk0)
    while keep.shape[0] > 1:
        keep, send = halve(keep, came)
        step *= 2
        came = swap(send, "seq", step)
    if relayed:
        messages = [[swap(first, "seq", 1)], [near, swap(near, "seq", 1)]]
        far, relay = after(far, send), after(relay, send)
        messages.append([far, swap(far, "seq", 1), relay, swap(relay, "seq", 1)])
    else:
        messages = joined(first, received, dk0, send)
    gk, gv = owned(some, messages[:-1], after(dk0, send), dv0, F32)
    mixed = call(mixed_kernel, [((tokens, width), BF16)], "mixed", 1, after(att, gk), w_out)[0]
    gk, gv = owned([last], messages[-1:], gk, gv, BF16)

    (gw,) = call(
        functools.partial(final_kernel, factor),
        [((own_rows, width), F32)],
        "total",
        1,
        after(keep, gk),
        came,
    )
    return (mixed[None], gq[None], gk[None], gv[None], gw)


def solution(mesh):
    rows = P("dp", "seq", None)
    return jax.shard_map(
        body,
        mesh=mesh,
        in_specs=(rows, rows, rows, rows, P()),
        out_specs=(rows, rows, rows, rows, P(("dp", "seq"), None)),
        check_vma=False,
    )
```

```python
import functools
import math

import jax
import jax.numpy as jnp
from jax import lax
from jax.experimental import pallas as pl
from jax.experimental.pallas import tpu as pltpu
from jax.sharding import PartitionSpec as P

HEADS = 8
HEAD_DIM = 128
BLOCK = 128
LANES = 128
SCALE = 1.0 / math.sqrt(HEAD_DIM)
SCALE2 = SCALE / math.log(2.0)
F32 = jnp.float32
BF16 = jnp.bfloat16
COST = 5_000_000_000
VMEM_LIMIT = 24 * 1024 * 1024


def dot(a, b, dims):
    return lax.dot_general(a, b, (dims, ((), ())), preferred_element_type=F32)


def nn(a, b):
    return dot(a, b, ((1,), (0,)))


def nt(a, b):
    return dot(a, b, ((1,), (1,)))


def tn(a, b):
    return dot(a, b, ((0,), (0,)))


def member(rows, cols, row_shift, col_shift, value):
    r = lax.broadcasted_iota(jnp.int32, (rows, cols), 0) >> row_shift
    c = lax.broadcasted_iota(jnp.int32, (rows, cols), 1) >> col_shift
    return jnp.where(r == c, value, 0.0).astype(BF16)


def call(kernel, outs, name, cost, *operands, scratch=(), space=pltpu.VMEM, limit=VMEM_LIMIT):
    return pl.pallas_call(
        kernel,
        name=name,
        out_shape=[jax.ShapeDtypeStruct(s, t) for s, t in outs],
        in_specs=[pl.BlockSpec(memory_space=space)] * len(operands),
        out_specs=[pl.BlockSpec(memory_space=pltpu.VMEM)] * len(outs),
        scratch_shapes=list(scratch),
        compiler_params=pltpu.CompilerParams(vmem_limit_bytes=limit),
        cost_estimate=pl.CostEstimate(flops=cost, bytes_accessed=1, transcendentals=0),
    )(*operands)


def pool_kernel(levels, k_ref, v_ref, *outs):
    tokens, width = k_ref.shape
    pools = [member(tokens >> l, tokens, 0, l, 0.5**l) for l in range(1, levels)]
    for i, src in enumerate((k_ref, v_ref)):
        x = src[...]
        for pool, out in zip(pools, outs):
            out[i] = nn(pool, x).astype(BF16)


def early_kernel(levels, q_ref, k_ref, v_ref, g_ref, w_ref, kv_ref, *refs):
    qhat_ref, gat_ref, e_ref, o_ref, stat_ref = refs[:5]
    qls = refs[5:]
    tokens, width = q_ref.shape
    q = q_ref[...]
    for l in range(1, levels):
        qhat_ref[l - 1] = nn(member(tokens, tokens, l, l, 0.5**l), q).astype(BF16)
        qls[l - 1][...] = nn(member(tokens >> l, tokens, 0, l, 0.5**l), q).astype(BF16)
    ones = jnp.ones((16, tokens + BLOCK), BF16)

    def attend(h, raw0, raw1):
        hs = slice(h * HEAD_DIM, (h + 1) * HEAD_DIM)
        top1 = jnp.max(raw1, axis=0, keepdims=True)
        top = jnp.max(raw0, axis=0, keepdims=True) * SCALE2
        top = jnp.maximum(top, top1 * SCALE2 + 1.0)
        e0 = jnp.exp2(raw0 * SCALE2 - top).astype(BF16)
        e1 = jnp.exp2(raw1 * SCALE2 + (1.0 - top)).astype(BF16)
        e_ref[h, :tokens, :] = e0
        e_ref[h, tokens:, :] = e1
        vals = jnp.concatenate([v_ref[:, hs], kv_ref[1, :, hs]], axis=0)
        both = nn(
            jnp.concatenate([vals.T, ones], axis=0), jnp.concatenate([e0, e1], axis=0)
        )
        o_ref[hs, :] = both[:HEAD_DIM]
        stat_ref[h : h + 1, :] = top
        stat_ref[HEADS + h : HEADS + h + 1, :] = both[HEAD_DIM : HEAD_DIM + 1]
        stat_ref[2 * HEADS + h : 2 * HEADS + h + 1, :] = top1

    def scores(h):
        hs = slice(h * HEAD_DIM, (h + 1) * HEAD_DIM)
        return nt(k_ref[:, hs], q_ref[:, hs]), nt(kv_ref[0, :, hs], qhat_ref[0, :, hs])

    g = g_ref[...]
    ahead = [scores(0), scores(1)]
    for h in range(HEADS):
        raws = ahead.pop(0)
        if h + 2 < HEADS:
            ahead.append(scores(h + 2))
        if h % 2 == 0:
            rows = slice(h * HEAD_DIM, (h + 2) * HEAD_DIM)
            gat_ref[rows, :] = nt(w_ref[rows, :], g).astype(BF16)
        attend(h, *raws)


def gathered(pieces, kvs, which, hs):
    out, at = [], 0
    for count in pieces:
        part = kvs[at : at + count]
        at += count
        out.append(jnp.concatenate([p[which, :, hs] for p in part], axis=0))
    return out


def forward_kernel(levels, pieces, dp, qhat_ref, gat_ref, o_ref, stat_ref, *refs):
    width, tokens = gat_ref.shape
    upper = levels - 1
    count = sum(pieces)
    qls, refs = refs[:upper], refs[upper:]
    kvs, refs = refs[:count], refs[count:]
    e_ref, grt_ref, grt0_ref, dd_ref, att_ref = refs[:5]
    blocks, msgs, aux_ref = refs[5 : 5 + dp], refs[5 + dp : -1], refs[-1]
    ones = jnp.ones((16, (upper - 1) * BLOCK), BF16)
    sums = [member(tokens >> l, tokens, 0, l, 1.0) for l in range(1, levels)]
    aux_ref[...] = jnp.zeros_like(aux_ref)

    def scores(h):
        hs = slice(h * HEAD_DIM, (h + 1) * HEAD_DIM)
        keys = gathered(pieces, kvs, 0, hs)
        return [nt(keys[l - 2], qhat_ref[l - 1, :, hs]) for l in range(2, levels)]

    def attend(h, raws):
        hs = slice(h * HEAD_DIM, (h + 1) * HEAD_DIM)
        tops = [jnp.max(raw, axis=0, keepdims=True) for raw in raws]
        top = stat_ref[h : h + 1, :]
        for l in range(2, levels):
            top = jnp.maximum(top, tops[l - 2] * SCALE2 + float(l))
        es = []
        for l, raw in enumerate(raws, 2):
            es.append(jnp.exp2(raw * SCALE2 + (float(l) - top)).astype(BF16))
            e_ref[h, (l - 2) * BLOCK : (l - 1) * BLOCK, :] = es[-1]
        vals = jnp.concatenate(gathered(pieces, kvs, 1, hs), axis=0)
        lhs = jnp.concatenate([vals.T, ones], axis=0)
        return top, tops, nn(lhs, jnp.concatenate(es, axis=0))

    def finish(h, top, tops, both):
        hs = slice(h * HEAD_DIM, (h + 1) * HEAD_DIM)
        a0 = jnp.exp2(stat_ref[h : h + 1, :] - top)
        den0 = stat_ref[HEADS + h : HEADS + h + 1, :]
        rden = 1.0 / (both[HEAD_DIM : HEAD_DIM + 1] + den0 * a0)
        att = ((both[:HEAD_DIM] + o_ref[hs, :] * a0) * rden).astype(BF16)
        att_ref[hs, :] = att
        grt = gat_ref[hs, :].astype(F32) * rden
        grt_ref[hs, :] = grt.astype(BF16)
        grt0_ref[hs, :] = (grt * a0).astype(BF16)
        delta = jnp.sum(grt * att.astype(F32), axis=0, keepdims=True)
        dd_ref[h : h + 1, :] = delta
        dd_ref[HEADS + h : HEADS + h + 1, :] = delta * a0
        tops = [stat_ref[2 * HEADS + h : 2 * HEADS + h + 1, :]] + tops
        for l in range(1, levels):
            mu = tops[l - 1].astype(BF16).astype(F32)
            a = jnp.exp2(mu * SCALE2 + (float(l) - top))
            msgs[l - 1][:, hs] = nt(sums[l - 1], (grt * a).astype(BF16)).astype(BF16)
            aux_ref[l - 1, h : h + 1, :] = mu * 0.5**l
            aux_ref[l - 1, HEADS + h : HEADS + h + 1, :] = delta * a

    ahead, behind = [scores(0), scores(1)], None
    for h in range(HEADS):
        raws = ahead.pop(0)
        if h + 2 < HEADS:
            ahead.append(scores(h + 2))
        state = attend(h, raws)
        if behind is not None:
            finish(h - 1, *behind)
        behind = state
    finish(HEADS - 1, *behind)
    me, core = lax.axis_index("dp"), lax.axis_index("seq") & 1
    span = width // dp
    for role in range(dp):
        at = pl.multiple_of((me ^ role_mask(role, core, dp)) * span, span)
        blocks[role][...] = att_ref[pl.ds(at, span), :]
    for l in range(1, levels):
        msgs[l - 1][:, width : 2 * width] = qls[l - 1][...]
        msgs[l - 1][:, 2 * width :] = nt(sums[l - 1], aux_ref[l - 1].astype(BF16)).astype(BF16)


def backward_kernel(levels, pieces, e0_ref, e_ref, grt0_ref, grt_ref, dd_ref, *refs):
    q_ref, k_ref, v_ref, kv_ref = refs[:4]
    tokens, width = q_ref.shape
    kvs, (gq_ref, dk_ref, dv_ref, y_ref) = refs[4:-4], refs[-4:]

    def probs(h):
        hs = slice(h * HEAD_DIM, (h + 1) * HEAD_DIM)
        vals0 = jnp.concatenate([v_ref[:, hs], kv_ref[1, :, hs]], axis=0)
        vals = jnp.concatenate(gathered(pieces, kvs, 1, hs), axis=0)
        return nn(vals0, grt0_ref[hs, :]), nn(vals, grt_ref[hs, :])

    def rest(h, dpt0, dpt):
        hs = slice(h * HEAD_DIM, (h + 1) * HEAD_DIM)
        e0 = e0_ref[h]
        ds0 = (e0.astype(F32) * (dpt0 - dd_ref[HEADS + h : HEADS + h + 1, :])).astype(BF16)
        ds = (e_ref[h].astype(F32) * (dpt - dd_ref[h : h + 1, :])).astype(BF16)
        keys = gathered(pieces, kvs, 0, hs)
        y_ref[hs, :tokens] = tn(k_ref[:, hs], ds0[:tokens]).astype(BF16)
        y_ref[hs, tokens : 2 * tokens] = tn(kv_ref[0, :, hs], ds0[tokens:]).astype(BF16)
        for l in range(2, levels):
            part = ds[(l - 2) * BLOCK : (l - 1) * BLOCK]
            y_ref[hs, l * tokens : (l + 1) * tokens] = tn(keys[l - 2], part).astype(BF16)
        dv_ref[:, hs] = nt(e0[:tokens], grt0_ref[hs, :]).astype(BF16)
        dk_ref[:, hs] = (nn(ds0[:tokens], q_ref[:, hs]) * SCALE).astype(BF16)

    ahead = [probs(0), probs(1)]
    for h in range(HEADS):
        now = ahead.pop(0)
        if h + 2 < HEADS:
            ahead.append(probs(h + 2))
        rest(h, *now)
    spread = jnp.concatenate(
        [member(tokens, tokens, l, l, 0.5**l) for l in range(levels)], axis=1
    )
    for c in range(0, width, 256):
        cs = slice(c, c + 256)
        gq_ref[:, cs] = (nt(spread, y_ref[cs, :]) * SCALE).astype(BF16)


def weight_kernel(dp, nz, *refs):
    atts, refs = refs[:dp], refs[dp:]
    grads, (keep_ref, even_ref, odd_ref, total_ref) = refs[:-4], refs[-4:]
    a = jnp.concatenate([x[...] for x in atts], axis=1)
    width = grads[0].shape[1]
    for c in range(0, width, 256):
        cs = slice(c, c + 256)
        g = jnp.concatenate([x[:, cs] for x in grads], axis=0)
        total_ref[:, cs] = nn(a, g)
    rows = total_ref.shape[0] // (2 * nz)
    seq = lax.axis_index("seq")
    core, z = seq & 1, seq >> 1
    for m in range(nz):
        base = (z ^ m) * 2 * rows
        mine = pl.multiple_of(base + core * rows, rows)
        other = pl.multiple_of(base + (1 - core) * rows, rows)
        keep_ref[m] = total_ref[pl.ds(mine, rows), :]
        send_ref = odd_ref if m % 2 else even_ref
        send_ref[m // 2] = total_ref[pl.ds(other, rows), :].astype(BF16)


def halve_kernel(count, keep_ref, *refs):
    got, (next_ref, send_ref) = refs[:count], refs[count:]

    def total(i):
        return keep_ref[i] + got[i % count][i // count].astype(F32)

    kept = next_ref.shape[0]
    for i in range(kept):
        next_ref[i] = total(i)
        send_ref[i] = total(kept + i).astype(BF16)


def mixed_kernel(att_ref, w_ref, out_ref):
    att = att_ref[...].T
    for c in range(0, w_ref.shape[1], 256):
        out_ref[:, c : c + 256] = nn(att, w_ref[:, c : c + 256]).astype(BF16)


def final_kernel(factor, keep_ref, got_ref, out_ref):
    out_ref[...] = (keep_ref[0] + got_ref[0].astype(F32)) * factor


def owner_kernel(chosen, pieces, tokens, *refs):
    kvs, refs = refs[: len(chosen)], refs[len(chosen) :]
    msgs, refs = refs[: sum(pieces)], refs[sum(pieces) :]
    dk0_ref, dv0_ref, gk_ref, gv_ref, dks_ref, dvs_ref = refs
    width = dk0_ref.shape[1]
    auxes, at = [], 0
    groups = []
    for count in pieces:
        part = msgs[at : at + count]
        at += count
        groups.append(part)
        auxes.append(
            jnp.concatenate([p[:, 2 * width : 2 * width + LANES] for p in part], axis=0)
        )
    lane = lax.broadcasted_iota(jnp.int32, (tokens >> 1, LANES), 1)

    def products(h):
        hs = slice(h * HEAD_DIM, (h + 1) * HEAD_DIM)
        qs = slice(width + h * HEAD_DIM, width + (h + 1) * HEAD_DIM)
        minus_mu = jnp.where(lane == h, -1.0, 0.0).astype(BF16)
        minus_d = jnp.where(lane == HEADS + h, -1.0, 0.0).astype(BF16)
        out = []
        for group, aux, kv, l in zip(groups, auxes, kvs, chosen):
            n = tokens >> l
            ga = jnp.concatenate([p[:, hs] for p in group], axis=0)
            q = jnp.concatenate([p[:, qs] for p in group], axis=0)
            k = jnp.concatenate([kv[0, :, hs], minus_mu[:n]], axis=1)
            v = jnp.concatenate([kv[1, :, hs], minus_d[:n]], axis=1)
            raw = nt(k, jnp.concatenate([q, aux], axis=1))
            out.append((ga, q, raw, nt(v, jnp.concatenate([ga, aux], axis=1))))
        return out

    def gradients(h, parts):
        hs = slice(h * HEAD_DIM, (h + 1) * HEAD_DIM)
        at = 0
        for ga, q, raw, dp_raw in parts:
            n = raw.shape[0]
            e = jnp.exp2(raw * SCALE2)
            ds = (e * dp_raw).astype(BF16)
            dvs_ref[at : at + n, hs] = nn(e.astype(BF16), ga).astype(BF16)
            dks_ref[at : at + n, hs] = (nn(ds, q) * SCALE).astype(BF16)
            at += n

    depth = 4
    ahead = [products(h) for h in range(depth)]
    for h in range(HEADS):
        parts = ahead.pop(0)
        if h + depth < HEADS:
            ahead.append(products(h + depth))
        gradients(h, parts)
    spread = jnp.concatenate([member(tokens, tokens >> l, l, 0, 0.5**l) for l in chosen], axis=1)
    for c in range(0, width, 256):
        cs = slice(c, c + 256)
        gk = dk0_ref[:, cs].astype(F32) + nn(spread, dks_ref[:, cs])
        gv = dv0_ref[:, cs].astype(F32) + nn(spread, dvs_ref[:, cs])
        gk_ref[:, cs] = gk.astype(gk_ref.dtype)
        gv_ref[:, cs] = gv.astype(gv_ref.dtype)


def after(x, *others):
    return lax.optimization_barrier((x, *others))[0]


def role_mask(role, core, dp):
    if dp != 4 or role % 3 == 0:
        return role
    return role + core if role == 1 else role - core


def exchange_role(x, role):
    dp, seq = lax.axis_size("dp"), lax.axis_size("seq")
    pairs = []
    for i in range(dp):
        for j in range(seq):
            pairs.append((i * seq + j, (i ^ role_mask(role, j & 1, dp)) * seq + j))
    return lax.ppermute(x, ("dp", "seq"), pairs)


def swap(x, axis, mask):
    count = lax.axis_size(axis)
    return lax.ppermute(x, axis, [(i, i ^ mask) for i in range(count)])


def body(queries, keys, values, grad_out, w_out):
    seq = lax.axis_size("seq")
    dp = lax.axis_size("dp")
    nz = seq // 2
    levels = seq.bit_length()
    upper = levels - 1
    q, k, v, g = queries[0], keys[0], values[0], grad_out[0]
    tokens, width = q.shape
    factor = 1.0 / math.sqrt(dp * seq * tokens)

    own = call(
        functools.partial(pool_kernel, levels),
        [((2, tokens >> l, width), BF16) for l in range(1, levels)],
        "pool",
        COST,
        k,
        v,
    )

    def across(per_level):
        return [
            (m.bit_length(), swap(per_level[m.bit_length()], "seq", 2 * m)) for m in range(1, nz)
        ]

    def joined(first, received, *wait):
        got = [[first]] + [[] for _ in range(upper - 1)]
        for at, x in received:
            x = after(x, *wait)
            got[at] += [x, swap(x, "seq", 1)]
        axis = first.ndim - 2
        return [x if x[0].shape[axis] >= 16 else [jnp.concatenate(x, axis=axis)] for x in got]

    kv1 = swap(own[0], "seq", 1)
    if nz == 4:
        through = swap(own[2], "seq", 4)
        received = [(1, swap(own[1], "seq", 2)), (2, through), (2, swap(through, "seq", 2))]
    else:
        received = across(own)

    early = call(
        functools.partial(early_kernel, levels),
        [
            ((upper, tokens, width), BF16),
            ((width, tokens), BF16),
            ((HEADS, tokens + BLOCK, tokens), BF16),
            ((width, tokens), F32),
            ((3 * HEADS, tokens), F32),
        ]
        + [((tokens >> l, width), BF16) for l in range(1, levels)],
        "early",
        1,
        after(q, own[0]),
        k,
        v,
        g,
        w_out,
        kv1,
    )
    qhat, gat, e0, o0, stats = early[:5]
    qls = early[5:]

    grads = [g] + [exchange_role(g, r) for r in range(1, min(dp, 3))]
    if dp == 4:
        grads.append(exchange_role(grads[1], 2))
    else:
        grads += [exchange_role(g, r) for r in range(3, dp)]

    stats = after(stats, grads[1])
    arrived = [x for _, x in received]
    arrived += [gat]
    pairs = joined(kv1, received, *arrived)[1:]
    pieces = [len(x) for x in pairs]
    flat = [x for part in pairs for x in part]

    outs = [
        ((HEADS, (upper - 1) * BLOCK, tokens), BF16),
        ((width, tokens), BF16),
        ((width, tokens), BF16),
        ((2 * HEADS, tokens), F32),
        ((width, tokens), BF16),
    ]
    outs += [((width // dp, tokens), BF16)] * dp
    outs += [((tokens >> l, 2 * width + LANES), BF16) for l in range(1, levels)]
    forward = call(
        functools.partial(forward_kernel, levels, pieces, dp),
        outs,
        "forward",
        1,
        qhat,
        gat,
        o0,
        stats,
        *qls,
        *flat,
        scratch=[pltpu.VMEM((upper, LANES, tokens), F32)],
    )
    e, grt, grt0, dd, att = forward[:5]
    blocks, outgoing = forward[5 : 5 + dp], forward[5 + dp :]

    atts = [blocks[0]] + [exchange_role(blocks[r], r) for r in range(1, dp)]
    relayed = nz == 4
    if relayed:
        far = swap(after(outgoing[2], *grads[3:4]), "seq", 4)
        near = swap(after(outgoing[1], *grads[3:]), "seq", 2)
    else:
        received = across(outgoing)

    rows = width // dp
    own_rows = rows // (2 * nz)
    mixed = call(mixed_kernel, [((tokens, width), BF16)], "mixed", COST, att, w_out)[0]
    atts[0] = after(atts[0], mixed)
    keep, even, odd = call(
        functools.partial(weight_kernel, dp, nz),
        [((nz, own_rows, width), F32)] + [((nz // 2, own_rows, width), BF16)] * 2,
        "weight",
        1,
        *atts,
        *grads,
        scratch=[pltpu.VMEM((rows, width), F32)],
    )

    def halve(keep, *got):
        n = keep.shape[0] // 2
        outs = [((n, own_rows, width), F32), ((n, own_rows, width), BF16)]
        return call(functools.partial(halve_kernel, len(got)), outs, "halve", 1, keep, *got)

    keep, send = halve(keep, swap(even, "seq", 1), swap(odd, "seq", 1))
    came = swap(send, "seq", nz)
    if relayed:
        relay = swap(after(far, keep), "seq", 2)
        near = after(near, keep)
    grt = after(grt, keep)

    gq, dk0, dv0 = call(
        functools.partial(backward_kernel, levels, pieces),
        [((tokens, width), BF16)] * 3,
        "backward",
        COST,
        e0,
        e,
        grt0,
        grt,
        dd,
        q,
        k,
        v,
        kv1,
        *flat,
        scratch=[pltpu.VMEM((width, levels * tokens), BF16)],
    )

    def owned(chosen, messages, dk, dv, dtype):
        flat = [x for part in messages for x in part]
        return call(
            functools.partial(owner_kernel, chosen, [len(x) for x in messages], tokens),
            [((tokens, width), dtype)] * 2,
            "owner",
            1,
            *[own[l - 1] for l in chosen],
            *flat,
            dk,
            dv,
            scratch=[pltpu.VMEM((sum(tokens >> l for l in chosen), width), BF16)] * 2,
        )

    last = levels - 1
    some = list(range(1, last))
    step = nz
    first = after(outgoing[0], keep)
    keep = after(keep, dk0)
    while keep.shape[0] > 1:
        keep, send = halve(keep, came)
        step //= 2
        came = swap(send, "seq", step)
    if relayed:
        messages = [[swap(first, "seq", 1)], [near, swap(near, "seq", 1)]]
        far, relay = after(far, send), after(relay, send)
        messages.append([far, swap(far, "seq", 1), relay, swap(relay, "seq", 1)])
    else:
        messages = joined(swap(first, "seq", 1), received, dk0, send)
    gk, gv = owned(some, messages[:-1], after(dk0, send), dv0, F32)
    gk, gv = owned([last], messages[-1:], gk, gv, BF16)

    (gw,) = call(
        functools.partial(final_kernel, factor),
        [((own_rows, width), F32)],
        "total",
        1,
        after(keep, gk),
        came,
    )
    return (mixed[None], gq[None], gk[None], gv[None], gw)


def solution(mesh):
    rows = P("dp", "seq", None)
    return jax.shard_map(
        body,
        mesh=mesh,
        in_specs=(rows, rows, rows, rows, P()),
        out_specs=(rows, rows, rows, rows, P(("dp", "seq"), None)),
        check_vma=False,
    )
```

```python
import functools
import math

import jax
import jax.numpy as jnp
from jax import lax
from jax.experimental import pallas as pl
from jax.experimental.pallas import tpu as pltpu
from jax.sharding import PartitionSpec as P

HEADS = 8
HEAD_DIM = 128
BLOCK = 128
LANES = 128
SCALE = 1.0 / math.sqrt(HEAD_DIM)
SCALE2 = SCALE / math.log(2.0)
F32 = jnp.float32
BF16 = jnp.bfloat16
COST = 5_000_000_000
VMEM_LIMIT = 24 * 1024 * 1024


def dot(a, b, dims):
    return lax.dot_general(a, b, (dims, ((), ())), preferred_element_type=F32)


def nn(a, b):
    return dot(a, b, ((1,), (0,)))


def nt(a, b):
    return dot(a, b, ((1,), (1,)))


def tn(a, b):
    return dot(a, b, ((0,), (0,)))


def member(rows, cols, row_shift, col_shift, value):
    r = lax.broadcasted_iota(jnp.int32, (rows, cols), 0) >> row_shift
    c = lax.broadcasted_iota(jnp.int32, (rows, cols), 1) >> col_shift
    return jnp.where(r == c, value, 0.0).astype(BF16)


def call(kernel, outs, name, cost, *operands, scratch=(), space=pltpu.VMEM, limit=VMEM_LIMIT):
    return pl.pallas_call(
        kernel,
        name=name,
        out_shape=[jax.ShapeDtypeStruct(s, t) for s, t in outs],
        in_specs=[pl.BlockSpec(memory_space=space)] * len(operands),
        out_specs=[pl.BlockSpec(memory_space=pltpu.VMEM)] * len(outs),
        scratch_shapes=list(scratch),
        compiler_params=pltpu.CompilerParams(vmem_limit_bytes=limit),
        cost_estimate=pl.CostEstimate(flops=cost, bytes_accessed=1, transcendentals=0),
    )(*operands)


def pool_kernel(levels, k_ref, v_ref, *outs):
    tokens, width = k_ref.shape
    pools = [member(tokens >> l, tokens, 0, l, 0.5**l) for l in range(1, levels)]
    for i, src in enumerate((k_ref, v_ref)):
        x = src[...]
        for pool, out in zip(pools, outs):
            out[i] = nn(pool, x).astype(BF16)


def early_kernel(levels, q_ref, k_ref, v_ref, g_ref, w_ref, kv_ref, *refs):
    qhat_ref, gat_ref, e_ref, o_ref, stat_ref = refs[:5]
    qls = refs[5:]
    tokens, width = q_ref.shape
    q = q_ref[...]
    for l in range(1, levels):
        qhat_ref[l - 1] = nn(member(tokens, tokens, l, l, 0.5**l), q).astype(BF16)
        qls[l - 1][...] = nn(member(tokens >> l, tokens, 0, l, 0.5**l), q).astype(BF16)
    ones = jnp.ones((16, tokens + BLOCK), BF16)

    def attend(h, raw0, raw1):
        hs = slice(h * HEAD_DIM, (h + 1) * HEAD_DIM)
        top1 = jnp.max(raw1, axis=0, keepdims=True)
        top = jnp.max(raw0, axis=0, keepdims=True) * SCALE2
        top = jnp.maximum(top, top1 * SCALE2 + 1.0)
        e0 = jnp.exp2(raw0 * SCALE2 - top).astype(BF16)
        e1 = jnp.exp2(raw1 * SCALE2 + (1.0 - top)).astype(BF16)
        e_ref[h, :tokens, :] = e0
        e_ref[h, tokens:, :] = e1
        vals = jnp.concatenate([v_ref[:, hs], kv_ref[1, :, hs]], axis=0)
        both = nn(
            jnp.concatenate([vals.T, ones], axis=0), jnp.concatenate([e0, e1], axis=0)
        )
        o_ref[hs, :] = both[:HEAD_DIM]
        stat_ref[h : h + 1, :] = top
        stat_ref[HEADS + h : HEADS + h + 1, :] = both[HEAD_DIM : HEAD_DIM + 1]
        stat_ref[2 * HEADS + h : 2 * HEADS + h + 1, :] = top1

    def scores(h):
        hs = slice(h * HEAD_DIM, (h + 1) * HEAD_DIM)
        return nt(k_ref[:, hs], q_ref[:, hs]), nt(kv_ref[0, :, hs], qhat_ref[0, :, hs])

    g = g_ref[...]
    ahead = [scores(0), scores(1)]
    for h in range(HEADS):
        raws = ahead.pop(0)
        if h + 2 < HEADS:
            ahead.append(scores(h + 2))
        if h % 2 == 0:
            rows = slice(h * HEAD_DIM, (h + 2) * HEAD_DIM)
            gat_ref[rows, :] = nt(w_ref[rows, :], g).astype(BF16)
        attend(h, *raws)


def gathered(pieces, kvs, which, hs):
    out, at = [], 0
    for count in pieces:
        part = kvs[at : at + count]
        at += count
        out.append(jnp.concatenate([p[which, :, hs] for p in part], axis=0))
    return out


def forward_kernel(levels, pieces, dp, qhat_ref, gat_ref, o_ref, stat_ref, *refs):
    width, tokens = gat_ref.shape
    upper = levels - 1
    count = sum(pieces)
    qls, refs = refs[:upper], refs[upper:]
    kvs, refs = refs[:count], refs[count:]
    e_ref, grt_ref, grt0_ref, dd_ref, att_ref = refs[:5]
    blocks, msgs, aux_ref = refs[5 : 5 + dp], refs[5 + dp : -1], refs[-1]
    ones = jnp.ones((16, (upper - 1) * BLOCK), BF16)
    sums = [member(tokens >> l, tokens, 0, l, 1.0) for l in range(1, levels)]
    aux_ref[...] = jnp.zeros_like(aux_ref)
    waiting = {}

    def scores(h):
        hs = slice(h * HEAD_DIM, (h + 1) * HEAD_DIM)
        keys = gathered(pieces, kvs, 0, hs)
        return [nt(keys[l - 2], qhat_ref[l - 1, :, hs]) for l in range(2, levels)]

    def attend(h, raws):
        hs = slice(h * HEAD_DIM, (h + 1) * HEAD_DIM)
        tops = [jnp.max(raw, axis=0, keepdims=True) for raw in raws]
        top = stat_ref[h : h + 1, :]
        for l in range(2, levels):
            top = jnp.maximum(top, tops[l - 2] * SCALE2 + float(l))
        es = []
        for l, raw in enumerate(raws, 2):
            es.append(jnp.exp2(raw * SCALE2 + (float(l) - top)).astype(BF16))
            e_ref[h, (l - 2) * BLOCK : (l - 1) * BLOCK, :] = es[-1]
        vals = jnp.concatenate(gathered(pieces, kvs, 1, hs), axis=0)
        lhs = jnp.concatenate([vals.T, ones], axis=0)
        return top, tops, nn(lhs, jnp.concatenate(es, axis=0))

    def finish(h, top, tops, both):
        hs = slice(h * HEAD_DIM, (h + 1) * HEAD_DIM)
        a0 = jnp.exp2(stat_ref[h : h + 1, :] - top)
        den0 = stat_ref[HEADS + h : HEADS + h + 1, :]
        rden = 1.0 / (both[HEAD_DIM : HEAD_DIM + 1] + den0 * a0)
        att = ((both[:HEAD_DIM] + o_ref[hs, :] * a0) * rden).astype(BF16)
        att_ref[hs, :] = att
        grt = gat_ref[hs, :].astype(F32) * rden
        grt_ref[hs, :] = grt.astype(BF16)
        grt0_ref[hs, :] = (grt * a0).astype(BF16)
        delta = jnp.sum(grt * att.astype(F32), axis=0, keepdims=True)
        dd_ref[h : h + 1, :] = delta
        dd_ref[HEADS + h : HEADS + h + 1, :] = delta * a0
        tops = [stat_ref[2 * HEADS + h : 2 * HEADS + h + 1, :]] + tops
        for l in range(1, levels):
            mu = tops[l - 1].astype(BF16).astype(F32)
            a = jnp.exp2(mu * SCALE2 + (float(l) - top))
            weighted = (grt * a).astype(BF16)
            if h % 2 == 0:
                waiting[l] = weighted
            else:
                pair = jnp.concatenate([waiting[l], weighted], axis=0)
                ps = slice((h - 1) * HEAD_DIM, (h + 1) * HEAD_DIM)
                msgs[l - 1][:, ps] = nt(sums[l - 1], pair).astype(BF16)
            aux_ref[l - 1, h : h + 1, :] = mu * 0.5**l
            aux_ref[l - 1, HEADS + h : HEADS + h + 1, :] = delta * a

    ahead, behind = [scores(0), scores(1), scores(2)], None
    for h in range(HEADS):
        raws = ahead.pop(0)
        if h + 3 < HEADS:
            ahead.append(scores(h + 3))
        state = attend(h, raws)
        if behind is not None:
            finish(h - 1, *behind)
        behind = state
    finish(HEADS - 1, *behind)
    me, core = lax.axis_index("dp"), lax.axis_index("seq") & 1
    span = width // dp
    for role in range(dp):
        at = pl.multiple_of((me ^ role_mask(role, core, dp)) * span, span)
        blocks[role][...] = att_ref[pl.ds(at, span), :]
    for l in range(1, levels):
        msgs[l - 1][:, width : 2 * width] = qls[l - 1][...]
        msgs[l - 1][:, 2 * width :] = nt(sums[l - 1], aux_ref[l - 1].astype(BF16)).astype(BF16)


def backward_kernel(levels, pieces, e0_ref, e_ref, grt0_ref, grt_ref, dd_ref, *refs):
    q_ref, k_ref, v_ref, kv_ref = refs[:4]
    tokens, width = q_ref.shape
    kvs, (gq_ref, dk_ref, dv_ref, y_ref) = refs[4:-4], refs[-4:]

    def probs(h):
        hs = slice(h * HEAD_DIM, (h + 1) * HEAD_DIM)
        vals0 = jnp.concatenate([v_ref[:, hs], kv_ref[1, :, hs]], axis=0)
        vals = jnp.concatenate(gathered(pieces, kvs, 1, hs), axis=0)
        return nn(vals0, grt0_ref[hs, :]), nn(vals, grt_ref[hs, :])

    def rest(h, dpt0, dpt):
        hs = slice(h * HEAD_DIM, (h + 1) * HEAD_DIM)
        e0 = e0_ref[h]
        ds0 = (e0.astype(F32) * (dpt0 - dd_ref[HEADS + h : HEADS + h + 1, :])).astype(BF16)
        ds = (e_ref[h].astype(F32) * (dpt - dd_ref[h : h + 1, :])).astype(BF16)
        keys = gathered(pieces, kvs, 0, hs)
        y_ref[hs, :tokens] = tn(k_ref[:, hs], ds0[:tokens]).astype(BF16)
        y_ref[hs, tokens : 2 * tokens] = tn(kv_ref[0, :, hs], ds0[tokens:]).astype(BF16)
        for l in range(2, levels):
            part = ds[(l - 2) * BLOCK : (l - 1) * BLOCK]
            y_ref[hs, l * tokens : (l + 1) * tokens] = tn(keys[l - 2], part).astype(BF16)
        dv_ref[:, hs] = nt(e0[:tokens], grt0_ref[hs, :]).astype(BF16)
        dk_ref[:, hs] = (nn(ds0[:tokens], q_ref[:, hs]) * SCALE).astype(BF16)

    ahead = [probs(0), probs(1)]
    for h in range(HEADS):
        now = ahead.pop(0)
        if h + 2 < HEADS:
            ahead.append(probs(h + 2))
        rest(h, *now)
    spread = jnp.concatenate(
        [member(tokens, tokens, l, l, 0.5**l) for l in range(levels)], axis=1
    )
    for c in range(0, width, 256):
        cs = slice(c, c + 256)
        gq_ref[:, cs] = (nt(spread, y_ref[cs, :]) * SCALE).astype(BF16)


def weight_kernel(dp, nz, *refs):
    atts, refs = refs[:dp], refs[dp:]
    grads, (keep_ref, even_ref, odd_ref, total_ref) = refs[:-4], refs[-4:]
    a = jnp.concatenate([x[...] for x in atts], axis=1)
    width = grads[0].shape[1]
    for c in range(0, width, 256):
        cs = slice(c, c + 256)
        g = jnp.concatenate([x[:, cs] for x in grads], axis=0)
        total_ref[:, cs] = nn(a, g)
    rows = total_ref.shape[0] // (2 * nz)
    seq = lax.axis_index("seq")
    core, z = seq & 1, seq >> 1
    for m in range(nz):
        base = (z ^ m) * 2 * rows
        mine = pl.multiple_of(base + core * rows, rows)
        other = pl.multiple_of(base + (1 - core) * rows, rows)
        keep_ref[m] = total_ref[pl.ds(mine, rows), :]
        send_ref = odd_ref if m % 2 else even_ref
        send_ref[m // 2] = total_ref[pl.ds(other, rows), :].astype(BF16)


def halve_kernel(count, keep_ref, *refs):
    got, (next_ref, send_ref) = refs[:count], refs[count:]

    def total(i):
        return keep_ref[i] + got[i % count][i // count].astype(F32)

    kept = next_ref.shape[0]
    for i in range(kept):
        next_ref[i] = total(i)
        send_ref[i] = total(kept + i).astype(BF16)


def mixed_kernel(att_ref, w_ref, out_ref):
    att = att_ref[...].T
    for c in range(0, w_ref.shape[1], 256):
        out_ref[:, c : c + 256] = nn(att, w_ref[:, c : c + 256]).astype(BF16)


def final_kernel(factor, keep_ref, got_ref, out_ref):
    out_ref[...] = (keep_ref[0] + got_ref[0].astype(F32)) * factor


def owner_kernel(chosen, pieces, tokens, *refs):
    kvs, refs = refs[: len(chosen)], refs[len(chosen) :]
    msgs, refs = refs[: sum(pieces)], refs[sum(pieces) :]
    dk0_ref, dv0_ref, gk_ref, gv_ref, dks_ref, dvs_ref = refs
    width = dk0_ref.shape[1]
    auxes, at = [], 0
    groups = []
    for count in pieces:
        part = msgs[at : at + count]
        at += count
        groups.append(part)
        auxes.append(
            jnp.concatenate([p[:, 2 * width : 2 * width + LANES] for p in part], axis=0)
        )
    lane = lax.broadcasted_iota(jnp.int32, (tokens >> 1, LANES), 1)

    def products(h):
        hs = slice(h * HEAD_DIM, (h + 1) * HEAD_DIM)
        qs = slice(width + h * HEAD_DIM, width + (h + 1) * HEAD_DIM)
        minus_mu = jnp.where(lane == h, -1.0, 0.0).astype(BF16)
        minus_d = jnp.where(lane == HEADS + h, -1.0, 0.0).astype(BF16)
        out = []
        for group, aux, kv, l in zip(groups, auxes, kvs, chosen):
            n = tokens >> l
            ga = jnp.concatenate([p[:, hs] for p in group], axis=0)
            q = jnp.concatenate([p[:, qs] for p in group], axis=0)
            k = jnp.concatenate([kv[0, :, hs], minus_mu[:n]], axis=1)
            v = jnp.concatenate([kv[1, :, hs], minus_d[:n]], axis=1)
            raw = nt(k, jnp.concatenate([q, aux], axis=1))
            out.append((ga, q, raw, nt(v, jnp.concatenate([ga, aux], axis=1))))
        return out

    def gradients(h, parts):
        hs = slice(h * HEAD_DIM, (h + 1) * HEAD_DIM)
        at = 0
        for ga, q, raw, dp_raw in parts:
            n = raw.shape[0]
            e = jnp.exp2(raw * SCALE2)
            ds = (e * dp_raw).astype(BF16)
            dvs_ref[at : at + n, hs] = nn(e.astype(BF16), ga).astype(BF16)
            dks_ref[at : at + n, hs] = (nn(ds, q) * SCALE).astype(BF16)
            at += n

    depth = 4
    ahead = [products(h) for h in range(depth)]
    for h in range(HEADS):
        parts = ahead.pop(0)
        if h + depth < HEADS:
            ahead.append(products(h + depth))
        gradients(h, parts)
    spread = jnp.concatenate([member(tokens, tokens >> l, l, 0, 0.5**l) for l in chosen], axis=1)
    for c in range(0, width, 256):
        cs = slice(c, c + 256)
        gk = dk0_ref[:, cs].astype(F32) + nn(spread, dks_ref[:, cs])
        gv = dv0_ref[:, cs].astype(F32) + nn(spread, dvs_ref[:, cs])
        gk_ref[:, cs] = gk.astype(gk_ref.dtype)
        gv_ref[:, cs] = gv.astype(gv_ref.dtype)


def after(x, *others):
    return lax.optimization_barrier((x, *others))[0]


def role_mask(role, core, dp):
    if dp != 4 or role % 3 == 0:
        return role
    return role + core if role == 1 else role - core


def exchange_role(x, role):
    dp, seq = lax.axis_size("dp"), lax.axis_size("seq")
    pairs = []
    for i in range(dp):
        for j in range(seq):
            pairs.append((i * seq + j, (i ^ role_mask(role, j & 1, dp)) * seq + j))
    return lax.ppermute(x, ("dp", "seq"), pairs)


def swap(x, axis, mask):
    count = lax.axis_size(axis)
    return lax.ppermute(x, axis, [(i, i ^ mask) for i in range(count)])


def body(queries, keys, values, grad_out, w_out):
    seq = lax.axis_size("seq")
    dp = lax.axis_size("dp")
    nz = seq // 2
    levels = seq.bit_length()
    upper = levels - 1
    q, k, v, g = queries[0], keys[0], values[0], grad_out[0]
    tokens, width = q.shape
    factor = 1.0 / math.sqrt(dp * seq * tokens)

    own = call(
        functools.partial(pool_kernel, levels),
        [((2, tokens >> l, width), BF16) for l in range(1, levels)],
        "pool",
        COST,
        k,
        v,
    )

    def across(per_level):
        return [
            (m.bit_length(), swap(per_level[m.bit_length()], "seq", 2 * m)) for m in range(1, nz)
        ]

    def joined(first, received, *wait):
        got = [[first]] + [[] for _ in range(upper - 1)]
        for at, x in received:
            x = after(x, *wait)
            got[at] += [x, swap(x, "seq", 1)]
        axis = first.ndim - 2
        return [x if x[0].shape[axis] >= 16 else [jnp.concatenate(x, axis=axis)] for x in got]

    kv1 = swap(own[0], "seq", 1)
    if nz == 4:
        through = swap(own[2], "seq", 4)
        received = [(1, swap(own[1], "seq", 2)), (2, through), (2, swap(through, "seq", 2))]
    else:
        received = across(own)

    early = call(
        functools.partial(early_kernel, levels),
        [
            ((upper, tokens, width), BF16),
            ((width, tokens), BF16),
            ((HEADS, tokens + BLOCK, tokens), BF16),
            ((width, tokens), F32),
            ((3 * HEADS, tokens), F32),
        ]
        + [((tokens >> l, width), BF16) for l in range(1, levels)],
        "early",
        1,
        after(q, own[0]),
        k,
        v,
        g,
        w_out,
        kv1,
    )
    qhat, gat, e0, o0, stats = early[:5]
    qls = early[5:]

    grads = [g] + [exchange_role(g, r) for r in range(1, min(dp, 3))]
    if dp == 4:
        grads.append(exchange_role(grads[1], 2))
    else:
        grads += [exchange_role(g, r) for r in range(3, dp)]

    stats = after(stats, grads[1])
    arrived = [x for _, x in received]
    arrived += [gat]
    pairs = joined(kv1, received, *arrived)[1:]
    pieces = [len(x) for x in pairs]
    flat = [x for part in pairs for x in part]

    outs = [
        ((HEADS, (upper - 1) * BLOCK, tokens), BF16),
        ((width, tokens), BF16),
        ((width, tokens), BF16),
        ((2 * HEADS, tokens), F32),
        ((width, tokens), BF16),
    ]
    outs += [((width // dp, tokens), BF16)] * dp
    outs += [((tokens >> l, 2 * width + LANES), BF16) for l in range(1, levels)]
    forward = call(
        functools.partial(forward_kernel, levels, pieces, dp),
        outs,
        "forward",
        1,
        qhat,
        gat,
        o0,
        stats,
        *qls,
        *flat,
        scratch=[pltpu.VMEM((upper, LANES, tokens), F32)],
    )
    e, grt, grt0, dd, att = forward[:5]
    blocks, outgoing = forward[5 : 5 + dp], forward[5 + dp :]

    atts = [blocks[0]] + [exchange_role(blocks[r], r) for r in range(1, dp)]
    relayed = nz == 4
    if relayed:
        far = swap(after(outgoing[2], *grads[3:4]), "seq", 4)
        near = swap(after(outgoing[1], *grads[3:]), "seq", 2)
    else:
        received = across(outgoing)

    rows = width // dp
    own_rows = rows // (2 * nz)
    mixed = call(mixed_kernel, [((tokens, width), BF16)], "mixed", COST, att, w_out)[0]
    atts[0] = after(atts[0], mixed)
    keep, even, odd = call(
        functools.partial(weight_kernel, dp, nz),
        [((nz, own_rows, width), F32)] + [((nz // 2, own_rows, width), BF16)] * 2,
        "weight",
        1,
        *atts,
        *grads,
        scratch=[pltpu.VMEM((rows, width), F32)],
    )

    def halve(keep, *got):
        n = keep.shape[0] // 2
        outs = [((n, own_rows, width), F32), ((n, own_rows, width), BF16)]
        return call(functools.partial(halve_kernel, len(got)), outs, "halve", 1, keep, *got)

    keep, send = halve(keep, swap(even, "seq", 1), swap(odd, "seq", 1))
    came = swap(send, "seq", nz)
    if relayed:
        relay = swap(after(far, keep), "seq", 2)
        near = after(near, keep)
    grt = after(grt, keep)

    gq, dk0, dv0 = call(
        functools.partial(backward_kernel, levels, pieces),
        [((tokens, width), BF16)] * 3,
        "backward",
        COST,
        e0,
        e,
        grt0,
        grt,
        dd,
        q,
        k,
        v,
        kv1,
        *flat,
        scratch=[pltpu.VMEM((width, levels * tokens), BF16)],
    )

    def owned(chosen, messages, dk, dv, dtype):
        flat = [x for part in messages for x in part]
        return call(
            functools.partial(owner_kernel, chosen, [len(x) for x in messages], tokens),
            [((tokens, width), dtype)] * 2,
            "owner",
            1,
            *[own[l - 1] for l in chosen],
            *flat,
            dk,
            dv,
            scratch=[pltpu.VMEM((sum(tokens >> l for l in chosen), width), BF16)] * 2,
        )

    last = levels - 1
    some = list(range(1, last))
    step = nz
    first = after(outgoing[0], keep)
    keep = after(keep, dk0)
    while keep.shape[0] > 1:
        keep, send = halve(keep, came)
        step //= 2
        came = swap(send, "seq", step)
    if relayed:
        messages = [[swap(first, "seq", 1)], [near, swap(near, "seq", 1)]]
        far, relay = after(far, send), after(relay, send)
        messages.append([far, swap(far, "seq", 1), relay, swap(relay, "seq", 1)])
    else:
        messages = joined(swap(first, "seq", 1), received, dk0, send)
    gk, gv = owned(some, messages[:-1], after(dk0, send), dv0, BF16)
    gk, gv = owned([last], messages[-1:], gk, gv, BF16)

    (gw,) = call(
        functools.partial(final_kernel, factor),
        [((own_rows, width), F32)],
        "total",
        1,
        after(keep, gk),
        came,
    )
    return (mixed[None], gq[None], gk[None], gv[None], gw)


def solution(mesh):
    rows = P("dp", "seq", None)
    return jax.shard_map(
        body,
        mesh=mesh,
        in_specs=(rows, rows, rows, rows, P()),
        out_specs=(rows, rows, rows, rows, P(("dp", "seq"), None)),
        check_vma=False,
    )
```

```python
import functools
import math

import jax
import jax.numpy as jnp
from jax import lax
from jax.experimental import pallas as pl
from jax.experimental.pallas import tpu as pltpu
from jax.sharding import PartitionSpec as P

HEADS = 8
HEAD_DIM = 128
BLOCK = 128
LANES = 128
SCALE = 1.0 / math.sqrt(HEAD_DIM)
SCALE2 = SCALE / math.log(2.0)
F32 = jnp.float32
BF16 = jnp.bfloat16
COST = 5_000_000_000
VMEM_LIMIT = 24 * 1024 * 1024


def dot(a, b, dims):
    return lax.dot_general(a, b, (dims, ((), ())), preferred_element_type=F32)


def nn(a, b):
    return dot(a, b, ((1,), (0,)))


def nt(a, b):
    return dot(a, b, ((1,), (1,)))


def tn(a, b):
    return dot(a, b, ((0,), (0,)))


def member(rows, cols, row_shift, col_shift, value):
    r = lax.broadcasted_iota(jnp.int32, (rows, cols), 0) >> row_shift
    c = lax.broadcasted_iota(jnp.int32, (rows, cols), 1) >> col_shift
    return jnp.where(r == c, value, 0.0).astype(BF16)


def call(kernel, outs, name, cost, *operands, scratch=(), space=pltpu.VMEM, limit=VMEM_LIMIT):
    return pl.pallas_call(
        kernel,
        name=name,
        out_shape=[jax.ShapeDtypeStruct(s, t) for s, t in outs],
        in_specs=[pl.BlockSpec(memory_space=space)] * len(operands),
        out_specs=[pl.BlockSpec(memory_space=pltpu.VMEM)] * len(outs),
        scratch_shapes=list(scratch),
        compiler_params=pltpu.CompilerParams(vmem_limit_bytes=limit),
        cost_estimate=pl.CostEstimate(flops=cost, bytes_accessed=1, transcendentals=0),
    )(*operands)


def pool_kernel(levels, k_ref, v_ref, *outs):
    tokens, width = k_ref.shape
    pools = [member(tokens >> l, tokens, 0, l, 0.5**l) for l in range(1, levels)]
    for i, src in enumerate((k_ref, v_ref)):
        x = src[...]
        for pool, out in zip(pools, outs):
            out[i] = nn(pool, x).astype(BF16)


def early_kernel(levels, q_ref, k_ref, v_ref, g_ref, w_ref, kv_ref, *refs):
    qhat_ref, gat_ref, e_ref, o_ref, stat_ref = refs[:5]
    qls = refs[5:]
    tokens, width = q_ref.shape
    q = q_ref[...]
    for l in range(1, levels):
        qhat_ref[l - 1] = nn(member(tokens, tokens, l, l, 0.5**l), q).astype(BF16)
        qls[l - 1][...] = nn(member(tokens >> l, tokens, 0, l, 0.5**l), q).astype(BF16)
    ones = jnp.ones((16, tokens + BLOCK), BF16)

    def attend(h, raw0, raw1):
        hs = slice(h * HEAD_DIM, (h + 1) * HEAD_DIM)
        top1 = jnp.max(raw1, axis=0, keepdims=True)
        top = jnp.max(raw0, axis=0, keepdims=True) * SCALE2
        top = jnp.maximum(top, top1 * SCALE2 + 1.0)
        e0 = jnp.exp2(raw0 * SCALE2 - top).astype(BF16)
        e1 = jnp.exp2(raw1 * SCALE2 + (1.0 - top)).astype(BF16)
        e_ref[h, :tokens, :] = e0
        e_ref[h, tokens:, :] = e1
        vals = jnp.concatenate([v_ref[:, hs], kv_ref[1, :, hs]], axis=0)
        both = nn(
            jnp.concatenate([vals.T, ones], axis=0), jnp.concatenate([e0, e1], axis=0)
        )
        o_ref[hs, :] = both[:HEAD_DIM]
        stat_ref[h : h + 1, :] = top
        stat_ref[HEADS + h : HEADS + h + 1, :] = both[HEAD_DIM : HEAD_DIM + 1]
        stat_ref[2 * HEADS + h : 2 * HEADS + h + 1, :] = top1

    def scores(h):
        hs = slice(h * HEAD_DIM, (h + 1) * HEAD_DIM)
        return nt(k_ref[:, hs], q_ref[:, hs]), nt(kv_ref[0, :, hs], qhat_ref[0, :, hs])

    g = g_ref[...]
    ahead = [scores(0), scores(1)]
    for h in range(HEADS):
        raws = ahead.pop(0)
        if h + 2 < HEADS:
            ahead.append(scores(h + 2))
        if h % 2 == 0:
            rows = slice(h * HEAD_DIM, (h + 2) * HEAD_DIM)
            gat_ref[rows, :] = nt(w_ref[rows, :], g).astype(BF16)
        attend(h, *raws)


def gathered(pieces, kvs, which, hs):
    out, at = [], 0
    for count in pieces:
        part = kvs[at : at + count]
        at += count
        out.append(jnp.concatenate([p[which, :, hs] for p in part], axis=0))
    return out


def forward_kernel(levels, pieces, dp, qhat_ref, gat_ref, o_ref, stat_ref, *refs):
    width, tokens = gat_ref.shape
    upper = levels - 1
    count = sum(pieces)
    qls, refs = refs[:upper], refs[upper:]
    kvs, refs = refs[:count], refs[count:]
    e_ref, grt_ref, grt0_ref, dd_ref, att_ref = refs[:5]
    blocks, msgs, aux_ref = refs[5 : 5 + dp], refs[5 + dp : -1], refs[-1]
    ones = jnp.ones((16, (upper - 1) * BLOCK), BF16)
    sums = [member(tokens >> l, tokens, 0, l, 1.0) for l in range(1, levels)]
    aux_ref[...] = jnp.zeros_like(aux_ref)
    waiting = {}

    def scores(h):
        hs = slice(h * HEAD_DIM, (h + 1) * HEAD_DIM)
        keys = gathered(pieces, kvs, 0, hs)
        return [nt(keys[l - 2], qhat_ref[l - 1, :, hs]) for l in range(2, levels)]

    def attend(h, raws):
        hs = slice(h * HEAD_DIM, (h + 1) * HEAD_DIM)
        tops = [jnp.max(raw, axis=0, keepdims=True) for raw in raws]
        top = stat_ref[h : h + 1, :]
        for l in range(2, levels):
            top = jnp.maximum(top, tops[l - 2] * SCALE2 + float(l))
        es = []
        for l, raw in enumerate(raws, 2):
            es.append(jnp.exp2(raw * SCALE2 + (float(l) - top)).astype(BF16))
            e_ref[h, (l - 2) * BLOCK : (l - 1) * BLOCK, :] = es[-1]
        vals = jnp.concatenate(gathered(pieces, kvs, 1, hs), axis=0)
        lhs = jnp.concatenate([vals.T, ones], axis=0)
        return top, tops, nn(lhs, jnp.concatenate(es, axis=0))

    def finish(h, top, tops, both):
        hs = slice(h * HEAD_DIM, (h + 1) * HEAD_DIM)
        a0 = jnp.exp2(stat_ref[h : h + 1, :] - top)
        den0 = stat_ref[HEADS + h : HEADS + h + 1, :]
        rden = 1.0 / (both[HEAD_DIM : HEAD_DIM + 1] + den0 * a0)
        att = ((both[:HEAD_DIM] + o_ref[hs, :] * a0) * rden).astype(BF16)
        att_ref[hs, :] = att
        grt = gat_ref[hs, :].astype(F32) * rden
        grt_ref[hs, :] = grt.astype(BF16)
        grt0_ref[hs, :] = (grt * a0).astype(BF16)
        delta = jnp.sum(grt * att.astype(F32), axis=0, keepdims=True)
        dd_ref[h : h + 1, :] = delta
        dd_ref[HEADS + h : HEADS + h + 1, :] = delta * a0
        tops = [stat_ref[2 * HEADS + h : 2 * HEADS + h + 1, :]] + tops
        for l in range(1, levels):
            mu = tops[l - 1].astype(BF16).astype(F32)
            a = jnp.exp2(mu * SCALE2 + (float(l) - top))
            weighted = (grt * a).astype(BF16)
            if h % 2 == 0:
                waiting[l] = weighted
            else:
                pair = jnp.concatenate([waiting[l], weighted], axis=0)
                ps = slice((h - 1) * HEAD_DIM, (h + 1) * HEAD_DIM)
                msgs[l - 1][:, ps] = nt(sums[l - 1], pair).astype(BF16)
            aux_ref[l - 1, h : h + 1, :] = mu * 0.5**l
            aux_ref[l - 1, HEADS + h : HEADS + h + 1, :] = delta * a

    ahead, behind = [scores(0), scores(1), scores(2)], None
    for h in range(HEADS):
        raws = ahead.pop(0)
        if h + 3 < HEADS:
            ahead.append(scores(h + 3))
        state = attend(h, raws)
        if behind is not None:
            finish(h - 1, *behind)
        behind = state
    finish(HEADS - 1, *behind)
    me, core = lax.axis_index("dp"), lax.axis_index("seq") & 1
    span = width // dp
    for role in range(dp):
        at = pl.multiple_of((me ^ role_mask(role, core, dp)) * span, span)
        blocks[role][...] = att_ref[pl.ds(at, span), :]
    for l in range(1, levels):
        msgs[l - 1][:, width : 2 * width] = qls[l - 1][...]
        msgs[l - 1][:, 2 * width :] = nt(sums[l - 1], aux_ref[l - 1].astype(BF16)).astype(BF16)


def backward_kernel(levels, pieces, e0_ref, e_ref, grt0_ref, grt_ref, dd_ref, *refs):
    q_ref, k_ref, v_ref, kv_ref = refs[:4]
    tokens, width = q_ref.shape
    kvs, (gq_ref, dk_ref, dv_ref, y_ref) = refs[4:-4], refs[-4:]

    def probs(h):
        hs = slice(h * HEAD_DIM, (h + 1) * HEAD_DIM)
        vals0 = jnp.concatenate([v_ref[:, hs], kv_ref[1, :, hs]], axis=0)
        vals = jnp.concatenate(gathered(pieces, kvs, 1, hs), axis=0)
        return nn(vals0, grt0_ref[hs, :]), nn(vals, grt_ref[hs, :])

    def rest(h, dpt0, dpt):
        hs = slice(h * HEAD_DIM, (h + 1) * HEAD_DIM)
        e0 = e0_ref[h]
        ds0 = (e0.astype(F32) * (dpt0 - dd_ref[HEADS + h : HEADS + h + 1, :])).astype(BF16)
        ds = (e_ref[h].astype(F32) * (dpt - dd_ref[h : h + 1, :])).astype(BF16)
        keys = gathered(pieces, kvs, 0, hs)
        y_ref[hs, :tokens] = tn(k_ref[:, hs], ds0[:tokens]).astype(BF16)
        y_ref[hs, tokens : 2 * tokens] = tn(kv_ref[0, :, hs], ds0[tokens:]).astype(BF16)
        for l in range(2, levels):
            part = ds[(l - 2) * BLOCK : (l - 1) * BLOCK]
            y_ref[hs, l * tokens : (l + 1) * tokens] = tn(keys[l - 2], part).astype(BF16)
        dv_ref[:, hs] = nt(e0[:tokens], grt0_ref[hs, :]).astype(BF16)
        dk_ref[:, hs] = (nn(ds0[:tokens], q_ref[:, hs]) * SCALE).astype(BF16)

    ahead = [probs(0), probs(1)]
    for h in range(HEADS):
        now = ahead.pop(0)
        if h + 2 < HEADS:
            ahead.append(probs(h + 2))
        rest(h, *now)
    spread = jnp.concatenate(
        [member(tokens, tokens, l, l, 0.5**l) for l in range(levels)], axis=1
    )
    for c in range(0, width, 256):
        cs = slice(c, c + 256)
        gq_ref[:, cs] = (nt(spread, y_ref[cs, :]) * SCALE).astype(BF16)


def weight_kernel(dp, nz, *refs):
    atts, refs = refs[:dp], refs[dp:]
    grads, (keep_ref, even_ref, odd_ref, total_ref) = refs[:-4], refs[-4:]
    a = jnp.concatenate([x[...] for x in atts], axis=1)
    width = grads[0].shape[1]
    for c in range(0, width, 256):
        cs = slice(c, c + 256)
        g = jnp.concatenate([x[:, cs] for x in grads], axis=0)
        total_ref[:, cs] = nn(a, g)
    rows = total_ref.shape[0] // (2 * nz)
    seq = lax.axis_index("seq")
    core, z = seq & 1, seq >> 1
    for m in range(nz):
        base = (z ^ m) * 2 * rows
        mine = pl.multiple_of(base + core * rows, rows)
        other = pl.multiple_of(base + (1 - core) * rows, rows)
        keep_ref[m] = total_ref[pl.ds(mine, rows), :]
        send_ref = odd_ref if m % 2 else even_ref
        send_ref[m // 2] = total_ref[pl.ds(other, rows), :].astype(BF16)


def halve_kernel(count, keep_ref, *refs):
    got, (next_ref, send_ref) = refs[:count], refs[count:]

    def total(i):
        return keep_ref[i] + got[i % count][i // count].astype(F32)

    kept = next_ref.shape[0]
    for i in range(kept):
        next_ref[i] = total(i)
        send_ref[i] = total(kept + i).astype(BF16)


def mixed_kernel(att_ref, w_ref, out_ref):
    att = att_ref[...].T
    for c in range(0, w_ref.shape[1], 256):
        out_ref[:, c : c + 256] = nn(att, w_ref[:, c : c + 256]).astype(BF16)


def owner_kernel(chosen, pieces, tokens, *refs):
    kvs, refs = refs[: len(chosen)], refs[len(chosen) :]
    msgs, refs = refs[: sum(pieces)], refs[sum(pieces) :]
    dk0_ref, dv0_ref, gk_ref, gv_ref, dks_ref, dvs_ref = refs
    width = dk0_ref.shape[1]
    auxes, at = [], 0
    groups = []
    for count in pieces:
        part = msgs[at : at + count]
        at += count
        groups.append(part)
        auxes.append(
            jnp.concatenate([p[:, 2 * width : 2 * width + LANES] for p in part], axis=0)
        )
    lane = lax.broadcasted_iota(jnp.int32, (tokens >> 1, LANES), 1)

    def products(h):
        hs = slice(h * HEAD_DIM, (h + 1) * HEAD_DIM)
        qs = slice(width + h * HEAD_DIM, width + (h + 1) * HEAD_DIM)
        minus_mu = jnp.where(lane == h, -1.0, 0.0).astype(BF16)
        minus_d = jnp.where(lane == HEADS + h, -1.0, 0.0).astype(BF16)
        out = []
        for group, aux, kv, l in zip(groups, auxes, kvs, chosen):
            n = tokens >> l
            ga = jnp.concatenate([p[:, hs] for p in group], axis=0)
            q = jnp.concatenate([p[:, qs] for p in group], axis=0)
            k = jnp.concatenate([kv[0, :, hs], minus_mu[:n]], axis=1)
            v = jnp.concatenate([kv[1, :, hs], minus_d[:n]], axis=1)
            raw = nt(k, jnp.concatenate([q, aux], axis=1))
            out.append((ga, q, raw, nt(v, jnp.concatenate([ga, aux], axis=1))))
        return out

    def gradients(h, parts):
        hs = slice(h * HEAD_DIM, (h + 1) * HEAD_DIM)
        at = 0
        for ga, q, raw, dp_raw in parts:
            n = raw.shape[0]
            e = jnp.exp2(raw * SCALE2)
            ds = (e * dp_raw).astype(BF16)
            dvs_ref[at : at + n, hs] = nn(e.astype(BF16), ga).astype(BF16)
            dks_ref[at : at + n, hs] = (nn(ds, q) * SCALE).astype(BF16)
            at += n

    depth = 4
    ahead = [products(h) for h in range(depth)]
    for h in range(HEADS):
        parts = ahead.pop(0)
        if h + depth < HEADS:
            ahead.append(products(h + depth))
        gradients(h, parts)
    spread = jnp.concatenate([member(tokens, tokens >> l, l, 0, 0.5**l) for l in chosen], axis=1)
    for c in range(0, width, 256):
        cs = slice(c, c + 256)
        gk = dk0_ref[:, cs].astype(F32) + nn(spread, dks_ref[:, cs])
        gv = dv0_ref[:, cs].astype(F32) + nn(spread, dvs_ref[:, cs])
        gk_ref[:, cs] = gk.astype(gk_ref.dtype)
        gv_ref[:, cs] = gv.astype(gv_ref.dtype)


def after(x, *others):
    return lax.optimization_barrier((x, *others))[0]


def role_mask(role, core, dp):
    if dp != 4 or role % 3 == 0:
        return role
    return role + core if role == 1 else role - core


def exchange_role(x, role):
    dp, seq = lax.axis_size("dp"), lax.axis_size("seq")
    pairs = []
    for i in range(dp):
        for j in range(seq):
            pairs.append((i * seq + j, (i ^ role_mask(role, j & 1, dp)) * seq + j))
    return lax.ppermute(x, ("dp", "seq"), pairs)


def swap(x, axis, mask):
    count = lax.axis_size(axis)
    return lax.ppermute(x, axis, [(i, i ^ mask) for i in range(count)])


def body(queries, keys, values, grad_out, w_out):
    seq = lax.axis_size("seq")
    dp = lax.axis_size("dp")
    nz = seq // 2
    levels = seq.bit_length()
    upper = levels - 1
    q, k, v, g = queries[0], keys[0], values[0], grad_out[0]
    tokens, width = q.shape
    factor = 1.0 / math.sqrt(dp * seq * tokens)

    own = call(
        functools.partial(pool_kernel, levels),
        [((2, tokens >> l, width), BF16) for l in range(1, levels)],
        "pool",
        COST,
        k,
        v,
    )

    def across(per_level):
        return [
            (m.bit_length(), swap(per_level[m.bit_length()], "seq", 2 * m)) for m in range(1, nz)
        ]

    def joined(first, received, *wait):
        got = [[first]] + [[] for _ in range(upper - 1)]
        for at, x in received:
            x = after(x, *wait)
            got[at] += [x, swap(x, "seq", 1)]
        axis = first.ndim - 2
        return [x if x[0].shape[axis] >= 16 else [jnp.concatenate(x, axis=axis)] for x in got]

    kv1 = swap(own[0], "seq", 1)
    if nz == 4:
        through = swap(own[2], "seq", 4)
        received = [(1, swap(own[1], "seq", 2)), (2, through), (2, swap(through, "seq", 2))]
    else:
        received = across(own)

    early = call(
        functools.partial(early_kernel, levels),
        [
            ((upper, tokens, width), BF16),
            ((width, tokens), BF16),
            ((HEADS, tokens + BLOCK, tokens), BF16),
            ((width, tokens), F32),
            ((3 * HEADS, tokens), F32),
        ]
        + [((tokens >> l, width), BF16) for l in range(1, levels)],
        "early",
        1,
        after(q, own[0]),
        k,
        v,
        g,
        w_out,
        kv1,
    )
    qhat, gat, e0, o0, stats = early[:5]
    qls = early[5:]

    grads = [g] + [exchange_role(g, r) for r in range(1, min(dp, 3))]
    if dp == 4:
        grads.append(exchange_role(grads[1], 2))
    else:
        grads += [exchange_role(g, r) for r in range(3, dp)]

    stats = after(stats, grads[1])
    arrived = [x for _, x in received]
    arrived += [gat]
    pairs = joined(kv1, received, *arrived)[1:]
    pieces = [len(x) for x in pairs]
    flat = [x for part in pairs for x in part]

    outs = [
        ((HEADS, (upper - 1) * BLOCK, tokens), BF16),
        ((width, tokens), BF16),
        ((width, tokens), BF16),
        ((2 * HEADS, tokens), F32),
        ((width, tokens), BF16),
    ]
    outs += [((width // dp, tokens), BF16)] * dp
    outs += [((tokens >> l, 2 * width + LANES), BF16) for l in range(1, levels)]
    forward = call(
        functools.partial(forward_kernel, levels, pieces, dp),
        outs,
        "forward",
        1,
        qhat,
        gat,
        o0,
        stats,
        *qls,
        *flat,
        scratch=[pltpu.VMEM((upper, LANES, tokens), F32)],
    )
    e, grt, grt0, dd, att = forward[:5]
    blocks, outgoing = forward[5 : 5 + dp], forward[5 + dp :]

    atts = [blocks[0]] + [exchange_role(blocks[r], r) for r in range(1, dp)]
    relayed = nz == 4
    if relayed:
        far = swap(after(outgoing[2], *grads[3:4]), "seq", 4)
        near = swap(after(outgoing[1], *grads[3:]), "seq", 2)
    else:
        received = across(outgoing)

    rows = width // dp
    own_rows = rows // (2 * nz)
    mixed = call(mixed_kernel, [((tokens, width), BF16)], "mixed", COST, att, w_out)[0]
    atts[0] = after(atts[0], mixed)
    keep, even, odd = call(
        functools.partial(weight_kernel, dp, nz),
        [((nz, own_rows, width), F32)] + [((nz // 2, own_rows, width), BF16)] * 2,
        "weight",
        1,
        *atts,
        *grads,
        scratch=[pltpu.VMEM((rows, width), F32)],
    )

    def halve(keep, *got):
        n = keep.shape[0] // 2
        outs = [((n, own_rows, width), F32), ((n, own_rows, width), BF16)]
        return call(functools.partial(halve_kernel, len(got)), outs, "halve", 1, keep, *got)

    keep, send = halve(keep, swap(even, "seq", 1), swap(odd, "seq", 1))
    came = swap(send, "seq", nz)
    if relayed:
        relay = swap(after(far, keep), "seq", 2)
        near = after(near, keep)
    grt = after(grt, keep)

    gq, dk0, dv0 = call(
        functools.partial(backward_kernel, levels, pieces),
        [((tokens, width), BF16)] * 3,
        "backward",
        COST,
        e0,
        e,
        grt0,
        grt,
        dd,
        q,
        k,
        v,
        kv1,
        *flat,
        scratch=[pltpu.VMEM((width, levels * tokens), BF16)],
    )

    def owned(chosen, messages, dk, dv, dtype):
        flat = [x for part in messages for x in part]
        return call(
            functools.partial(owner_kernel, chosen, [len(x) for x in messages], tokens),
            [((tokens, width), dtype)] * 2,
            "owner",
            1,
            *[own[l - 1] for l in chosen],
            *flat,
            dk,
            dv,
            scratch=[pltpu.VMEM((sum(tokens >> l for l in chosen), width), BF16)] * 2,
        )

    last = levels - 1
    some = list(range(1, last))
    step = nz
    first = after(outgoing[0], keep)
    keep = after(keep, dk0)
    while keep.shape[0] > 1:
        keep, send = halve(keep, came)
        step //= 2
        came = swap(send, "seq", step)
    if relayed:
        messages = [[swap(first, "seq", 1)], [near, swap(near, "seq", 1)]]
        far, relay = after(far, send), after(relay, send)
        messages.append([far, swap(far, "seq", 1), relay, swap(relay, "seq", 1)])
    else:
        messages = joined(swap(first, "seq", 1), received, dk0, send)
    gk, gv = owned(some, messages[:-1], after(dk0, send), dv0, BF16)
    gk, gv = owned([last], messages[-1:], gk, gv, BF16)

    gw = (after(keep, gk)[0] + came[0].astype(F32)) * factor
    return (mixed[None], gq[None], gk[None], gv[None], gw)


def solution(mesh):
    rows = P("dp", "seq", None)
    return jax.shard_map(
        body,
        mesh=mesh,
        in_specs=(rows, rows, rows, rows, P()),
        out_specs=(rows, rows, rows, rows, P(("dp", "seq"), None)),
        check_vma=False,
    )
```
